32 devices in a mesh: section: 2 (over core), tensor: 4 (over y, x), dp: 4 (over z).
Axes of the slice: x: 2, y: 2, z: 4, core: 2. Of those that a mesh axis runs over, the one named last changes fastest.
Arguments:
- x_in: bfloat16 [3, 4096, 1152], P(None, ('dp', 'tensor')), may hold values from -6 to 6
- cotangent: bfloat16 [3, 4096, 1152], P(None, ('dp', 'tensor')), may hold values from -6 to 6
- cond: bfloat16 [3, 32, 1152], P(None, 'dp'), may hold values from -6 to 6
- crop_len: int32 [3, 32], P(None, 'dp'), may hold values from 0 to 512, as said below
- head_mask: int32 [3, 32, 16], P(None, 'dp', 'tensor'), may hold values 0 or 1
- skip_mask: int32 [3, 4096], P(None, 'dp'), may hold values 0 or 1
- ada_w: bfloat16 [2, 1152, 6912], P('section', None, 'tensor'), may hold values from -0.1875 to 0.1875
- qkv_w: bfloat16 [2, 3, 1152, 1152], P('section', None, None, 'tensor'), may hold values from -0.1875 to 0.1875
- proj_w: bfloat16 [2, 1152, 1152], P('section', 'tensor'), may hold values from -1.5 to 1.5
- fc1_w: bfloat16 [2, 1152, 4608], P('section', None, 'tensor'), may hold values from -0.1875 to 0.1875
- fc2_w: bfloat16 [2, 4608, 1152], P('section', 'tensor'), may hold values from -0.09375 to 0.09375
Outputs:
- residual: float32 [2, 3, 4096, 1152], P('section', None, ('dp', 'tensor'))
- input_grad: bfloat16 [2, 3, 4096, 1152], P('section', None, ('dp', 'tensor'))
- sublayer_rms: float32 [2, 2, 3, 4096], P('section', None, None, ('dp', 'tensor'))
- ada_grad: float32 [2, 1152, 6912], P('section', 'dp', 'tensor')
- qkv_grad: float32 [2, 3, 1152, 1152], P('section', None, 'dp', 'tensor')
- proj_grad: float32 [2, 1152, 1152], P('section', 'tensor', 'dp')
- fc1_grad: float32 [2, 1152, 4608], P('section', 'dp', 'tensor')
- fc2_grad: float32 [2, 4608, 1152], P('section', 'tensor', 'dp')
The draws below stay inside these ranges and needn't reach their ends.
Inputs may be any that keep to these rules, and one draw needn't show every extreme that they name: `crop_len`: A row's crops fill its first slots in order from the row's start, later slots hold 0; a crop has 128 to 512 tokens, a row's lengths sum to at most 1024, and every micro-batch has a crop of exactly 512 tokens.
All inputs are finite; a program needn't handle non-finite values. No bound on the sum of `head_mask` or of `skip_mask` on one device may be relied on, other than what follows from the above.
Results may differ from the reference program's by a relative error of at most 0.033.
The reference program's roundings to bfloat16 on the way count: a program that leaves them out, or rounds other values in their place, can miss the bound.
Values may be sent and summed in bfloat16 or wider, within the bound.
No kernel may reach another device: no remote copies, remote signals or barrier semaphores. Data moves between devices by JAX's collectives and lax.ppermute only.
A program may use at most 320 MiB of HBM per device.

```python
import jax
import jax.numpy as jnp
from jax import lax

D = 1152
H = 16
FF = 4608
ROW = 1024
SLOTS = 8
CROP_MIN = 128
CROP_MAX = 512
MICRO = 3
TOKENS = 4096
CROPS = 32


def draw_crop_len(key, part):
    groups = CROPS // SLOTS
    count = MICRO * groups
    first_key = jax.random.fold_in(key, 11)
    second_key = jax.random.fold_in(key, 12)
    lengths = jax.random.randint(first_key, (count, SLOTS), CROP_MIN, CROP_MAX + 1).astype(jnp.int32)
    chosen = jax.random.randint(second_key, (MICRO,), 0, groups).astype(jnp.int32)
    row_group = jnp.arange(count, dtype=jnp.int32) % groups
    row_micro = jnp.arange(count, dtype=jnp.int32) // groups
    forced = row_group == chosen[row_micro]
    lead = jnp.where(forced, jnp.int32(CROP_MAX), lengths[:, 0])
    lengths = jnp.concatenate([lead[:, None], lengths[:, 1:]], axis=1)
    finish = jnp.cumsum(lengths, axis=1)
    lengths = jnp.where(finish <= ROW, lengths, 0).astype(jnp.int32)
    return lengths.reshape(MICRO, CROPS)


def with_ends(array, key, least, top_value):
    shape = array.shape
    index_at = [jax.random.randint(jax.random.fold_in(key, axis), (), 0, shape[axis]) for axis in range(len(shape))]
    array = array.at[tuple(index_at)].set(least)
    longest = shape.index(max(shape))
    index_at[longest] = (index_at[longest] + 1) % shape[longest]
    return array.at[tuple(index_at)].set(top_value)


def levels(stream_key, dims, pieces, low, high):
    def one(dim, parts):
        steps = jax.random.uniform(jax.random.fold_in(jax.random.fold_in(stream_key, 6), dim), (parts,), jnp.float32, low / len(pieces), high / len(pieces))
        return jnp.repeat(jnp.exp(steps), dims[dim] // parts).reshape((-1,) + (1,) * (len(dims) - dim - 1))

    loudness = one(*pieces[0])
    for cut in pieces[1:]:
        loudness = loudness * one(*cut)
    return loudness


def gaussian(rng, dims, deviation, most, shards=(), held_as=jnp.bfloat16):
    gain = levels(rng, dims, shards, -0.22, 0.18) if shards else 1.0
    array = jax.random.normal(rng, dims, jnp.float32) * deviation * gain
    return jnp.minimum(jnp.maximum(array, -most), most).astype(held_as)


def setup_inputs(seed: int = 0) -> dict:
    arg_keys = jax.random.split(jax.random.key(seed), 12)
    x_in = gaussian(arg_keys[0], (MICRO, TOKENS, D), 1.0, 6.0, ((1, 16),))
    cotangent = gaussian(arg_keys[1], (MICRO, TOKENS, D), 1.0, 6.0, ((1, 16),))
    cond = gaussian(arg_keys[2], (MICRO, CROPS, D), 1.0, 6.0, ((1, 4),))
    crop_len = draw_crop_len(jax.random.fold_in(arg_keys[11], 71), 0)
    head_mask = with_ends((jax.random.randint(arg_keys[4], (MICRO, CROPS, H), 0, 4) < 3).astype(jnp.int32), jax.random.fold_in(arg_keys[4], 1), 0, 1)
    skip_mask = with_ends((jax.random.randint(arg_keys[5], (MICRO, TOKENS), 0, 3) < 2).astype(jnp.int32), jax.random.fold_in(arg_keys[5], 1), 0, 1)
    ada_w = gaussian(arg_keys[6], (2, D, 6 * D), D ** -0.5, 0.1875, ((0, 2), (2, 4)))
    qkv_w = gaussian(arg_keys[7], (2, 3, D, D), D ** -0.5, 0.1875, ((0, 2), (3, 4)))
    proj_w = gaussian(arg_keys[8], (2, D, D), (D // 64) ** -0.5, 1.5, ((0, 2), (1, 4)))
    fc1_w = gaussian(arg_keys[9], (2, D, FF), D ** -0.5, 0.1875, ((0, 2), (2, 4)))
    fc2_w = gaussian(arg_keys[10], (2, FF, D), FF ** -0.5, 0.09375, ((0, 2), (1, 4)))
    return {"x_in": x_in, "cotangent": cotangent, "cond": cond, "crop_len": crop_len, "head_mask": head_mask, "skip_mask": skip_mask, "ada_w": ada_w, "qkv_w": qkv_w, "proj_w": proj_w, "fc1_w": fc1_w, "fc2_w": fc2_w}


highest = lax.Precision.HIGHEST
epsilon = 1e-06

@jax.custom_vjp
def low(v):
    return lax.optimization_barrier(v.astype(jnp.bfloat16)).astype(jnp.float32)

@jax.custom_vjp
def low_back(v):
    return v

def low_keep(v):
    return (low(v), None)

def low_pass(kept, grad):
    return (grad,)

def back_keep(v):
    return (v, None)

def back_low(kept, grad):
    return (low(grad),)
low.defvjp(low_keep, low_pass)
low_back.defvjp(back_keep, back_low)

def both_ways(value):
    return low(low_back(value))

def normalize(value):
    centered = value - lax.optimization_barrier(jnp.mean(value, axis=-1, keepdims=True))
    return centered * lax.rsqrt(lax.optimization_barrier(jnp.mean(centered * centered, axis=-1, keepdims=True)) + epsilon)

def crop_layout(lengths, rows):
    places = jnp.arange(rows, dtype=jnp.int32)
    finish = jnp.cumsum(lengths).astype(jnp.int32)
    begin = (finish - lengths).astype(jnp.int32)
    inside = (places[:, None] >= begin[None, :]) & (places[:, None] < finish[None, :])
    count = lengths.shape[0]
    flags = inside.astype(jnp.int32)
    labels = lax.optimization_barrier(jnp.sum(flags * jnp.arange(count, dtype=jnp.int32)[None, :], axis=1))
    labels = labels + (1 - lax.optimization_barrier(jnp.sum(flags, axis=1))) * count
    return (inside.astype(jnp.float32), labels)

def layer_row(params, x, cond, lengths, hmask, skip):
    ada, wqkv, wproj, wup, wdown = params
    rows, width = x.shape
    heads = hmask.shape[1]
    head_dim = width // heads
    member, labels = crop_layout(lengths, rows)
    condition = low(jax.nn.silu(cond))
    modulation = jnp.dot(condition, ada, precision=highest)
    per_token = jnp.dot(member, modulation, precision=highest)
    shift_one, scale_one, gate_one, shift_two, scale_two, gate_two = jnp.split(per_token, 6, axis=1)
    first = low(normalize(x) * (1.0 + scale_one) + shift_one)
    project = both_ways(jnp.einsum('nd,cde->cne', first, wqkv, precision=highest))
    query = project[0].reshape(rows, heads, head_dim)
    keys = project[1].reshape(rows, heads, head_dim)
    values = project[2].reshape(rows, heads, head_dim)
    scores = low_back(jnp.einsum('qhe,khe->hqk', query, keys, precision=highest) * head_dim ** (-0.5))
    same = labels[:, None] == labels[None, :]
    scores = jnp.where(same[None], scores, -1e+30)
    weights = low(jax.nn.softmax(scores, axis=-1))
    mixed = jnp.einsum('hqk,khe->qhe', weights, values, precision=highest)
    token_heads = jnp.dot(member, hmask, precision=highest)
    mixed = both_ways((mixed * token_heads[:, :, None]).reshape(rows, width))
    attended = low_back(jnp.dot(mixed, wproj, precision=highest))
    middle = x + gate_one * attended
    second = low(normalize(middle) * (1.0 + scale_two) + shift_two)
    hidden_pre = low_back(jnp.dot(second, wup, precision=highest))
    hidden = low(jax.nn.gelu(hidden_pre, approximate=True) * skip[:, None])
    feed = low_back(jnp.dot(hidden, wdown, precision=highest))
    output = middle + gate_two * feed
    squares = jnp.stack([lax.optimization_barrier(jnp.mean(attended * attended, axis=1)), lax.optimization_barrier(jnp.mean(feed * feed, axis=1))])
    return (output, squares)

def run_section(params, rows_x, conds, lengths, hmask, skip):

    def one(items):
        return jax.checkpoint(layer_row)(params, *items)
    return lax.map(one, (rows_x, conds, lengths, hmask, skip))

def reference(x_in, cotangent, cond, crop_len, head_mask, skip_mask, ada_w, qkv_w, proj_w, fc1_w, fc2_w):
    micro = x_in.shape[0]
    groups = x_in.shape[1] // ROW
    count = micro * groups
    rows_x = x_in.astype(jnp.float32).reshape(count, ROW, D)
    conds = cond.astype(jnp.float32).reshape(count, SLOTS, D)
    lengths = crop_len.reshape(count, SLOTS).astype(jnp.int32)
    hmask = head_mask.astype(jnp.float32).reshape(count, SLOTS, H)
    skip = skip_mask.astype(jnp.float32).reshape(count, ROW)
    stacks = (ada_w, qkv_w, proj_w, fc1_w, fc2_w)
    params_zero = tuple((w[0].astype(jnp.float32) for w in stacks))
    params_one = tuple((w[1].astype(jnp.float32) for w in stacks))

    def section_fn(params, inputs):
        return run_section(params, inputs, conds, lengths, hmask, skip)
    out_zero, pull_zero, squares_zero = jax.vjp(section_fn, params_zero, rows_x, has_aux=True)
    out_one, pull_one, squares_one = jax.vjp(section_fn, params_one, out_zero, has_aux=True)
    grads_one, back_one = pull_one(cotangent.astype(jnp.float32).reshape(count, ROW, D))
    grads_zero, back_zero = pull_zero(back_one)
    residual = jnp.stack([out_zero, out_one]).reshape(2, micro, groups * ROW, D)
    input_grad = jnp.stack([back_zero.astype(jnp.bfloat16), back_one.astype(jnp.bfloat16)]).reshape(2, micro, groups * ROW, D)

    def rms_of(squares):
        return jnp.transpose(jnp.sqrt(squares), (1, 0, 2)).reshape(2, micro, groups * ROW)
    sublayer_rms = jnp.stack([rms_of(squares_zero), rms_of(squares_one)])
    stacked = [jnp.stack([grads_zero[i], grads_one[i]]) for i in range(5)]
    return (residual, input_grad, sublayer_rms, stacked[0], stacked[1], stacked[2], stacked[3], stacked[4])
```

```python
import functools
import math

import jax
import jax.numpy as jnp
from jax import lax
from jax.experimental import pallas as pl
from jax.experimental.pallas import tpu as pltpu
from jax.sharding import PartitionSpec as P

highest = lax.Precision.HIGHEST
epsilon = 1e-06
f32 = jnp.float32
bf16 = jnp.bfloat16
log2e = math.log2(math.e)
kernel_vmem = 48 * 1024 * 1024


def normalize_keep(value):
    centered = value - jnp.mean(value, axis=-1, keepdims=True)
    factor = lax.rsqrt(jnp.mean(centered * centered, axis=-1, keepdims=True) + epsilon)
    return (centered * factor, factor)


def normalize_back(normed, factor, upstream):
    return factor * (
        upstream
        - jnp.mean(upstream, axis=-1, keepdims=True)
        - normed * jnp.mean(upstream * normed, axis=-1, keepdims=True)
    )


def swap_cores(block):
    return lax.ppermute(block, "section", [(0, 1), (1, 0)])


def along_x(block):
    return lax.ppermute(block, "tensor", [(0, 1), (1, 0), (2, 3), (3, 2)])


def along_y(block):
    return lax.ppermute(block, "tensor", [(0, 2), (2, 0), (1, 3), (3, 1)])


def square():
    return lax.axis_size("tensor") == 4


def half_order():
    if square():
        return [(0, 0), (2, 0), (0, 1), (1, 1), (1, 0), (3, 0), (2, 1), (3, 1)]
    return [(chunk, half) for chunk in range(lax.axis_size("tensor")) for half in (0, 1)]


def gather_rows(block):
    if not square():
        return lax.all_gather(block, "tensor", axis=0, tiled=True)
    half = block.shape[0] // 2
    from_x = along_x(block)
    from_y = along_y(block)
    far_first = along_y(from_x[:half])
    far_second = along_x(from_y[half:])
    return jnp.concatenate(
        [
            block[:half],
            from_y[:half],
            block[half:],
            from_x[half:],
            from_x[:half],
            far_first,
            from_y[half:],
            far_second,
        ],
        axis=0,
    )


def scatter_rows(partial):
    if not square():
        return lax.psum_scatter(partial, "tensor", scatter_dimension=0, tiled=True).astype(f32)
    half = partial.shape[0] // 8
    sum_x = partial[: 2 * half].astype(f32) + along_x(partial[4 * half : 6 * half]).astype(f32)
    sum_y = partial[2 * half : 4 * half].astype(f32) + along_y(partial[6 * half :]).astype(f32)
    first = sum_x[:half] + along_y(sum_x[half:].astype(bf16)).astype(f32)
    second = sum_y[:half] + along_x(sum_y[half:].astype(bf16)).astype(f32)
    return jnp.concatenate([first, second], axis=0)


def gather_columns(block):
    if not square():
        return lax.all_gather(block, "tensor", axis=1, tiled=True)
    from_x = along_x(block)
    from_y = along_y(block)
    pieces = jnp.stack([block, from_x, from_y, along_x(from_y)])
    here = lax.axis_index("tensor")
    return jnp.concatenate(
        [lax.dynamic_index_in_dim(pieces, here ^ j, 0, keepdims=False) for j in range(4)], axis=1
    )


def scatter_columns(partial):
    if not square():
        return lax.psum_scatter(partial, "tensor", scatter_dimension=1, tiled=True)
    here = lax.axis_index("tensor")
    columns = partial.shape[1] // 4

    def piece(distance):
        return lax.dynamic_slice_in_dim(partial, (here ^ distance) * columns, columns, 1)

    arrived = along_x(jnp.stack([piece(1), piece(3)]))
    return piece(0) + arrived[0] + along_y(piece(2) + arrived[1])


def gather_dp(block):
    size = lax.axis_size("dp")
    others = [
        lax.ppermute(block, "dp", [(i, (i + step) % size) for i in range(size)])
        for step in range(1, size)
    ]
    return jnp.stack([block] + others)


def dot_last(left, right):
    return lax.dot_general(left, right, (((1,), (1,)), ((), ())), preferred_element_type=f32)


def dot_plain(left, right):
    return lax.dot_general(left, right, (((1,), (0,)), ((), ())), preferred_element_type=f32)


def dot_first(left, right):
    return lax.dot_general(left, right, (((0,), (0,)), ((), ())), preferred_element_type=f32)


def attention_forward_kernel(
    heads, dim, own_ref, other_ref, label_ref, key_label_ref, mask_ref, mixed_ref, lse_ref
):
    rows = own_ref.shape[0]
    cols = heads * dim
    scale = dim ** (-0.5)
    labels = label_ref[...]
    same = [labels == key_label_ref[:, :rows], labels == key_label_ref[:, rows:]]
    mixed = []
    totals = []
    for head in range(heads):
        lo = head * dim
        query = own_ref[:, lo : lo + dim]
        keys = [own_ref[:, cols + lo : cols + lo + dim], other_ref[:, lo : lo + dim]]
        values = [
            own_ref[:, 2 * cols + lo : 2 * cols + lo + dim],
            other_ref[:, cols + lo : cols + lo + dim],
        ]
        scores = [jnp.where(same[j], dot_last(query, keys[j]), -1e30) for j in range(2)]
        peak = jnp.maximum(
            jnp.max(scores[0], axis=1, keepdims=True), jnp.max(scores[1], axis=1, keepdims=True)
        )
        expos = [jnp.exp2((scores[j] - peak) * (scale * log2e)) for j in range(2)]
        total = jnp.sum(expos[0], axis=1, keepdims=True) + jnp.sum(expos[1], axis=1, keepdims=True)
        inverse = 1.0 / total
        out = dot_plain((expos[0] * inverse).astype(bf16), values[0])
        out = out + dot_plain((expos[1] * inverse).astype(bf16), values[1])
        mixed.append((out * mask_ref[:, head : head + 1]).astype(bf16))
        totals.append(peak * scale + jnp.log(total))
    mixed_ref[...] = jnp.concatenate(mixed, axis=1)
    lse_ref[...] = jnp.concatenate(totals, axis=1)


def attention_forward(own, other, label_column, key_label_row, head_gate, heads):
    rows = own.shape[0]
    cols = own.shape[1] // 3
    return pl.pallas_call(
        functools.partial(attention_forward_kernel, heads, cols // heads),
        out_shape=(
            jax.ShapeDtypeStruct((rows, cols), bf16),
            jax.ShapeDtypeStruct((rows, heads), f32),
        ),
        compiler_params=pltpu.CompilerParams(vmem_limit_bytes=kernel_vmem),
        cost_estimate=pl.CostEstimate(
            flops=8 * rows * rows * cols,
            bytes_accessed=2 * rows * cols * 6,
            transcendentals=2 * rows * rows * heads,
        ),
        name="attend",
    )(own, other, label_column, key_label_row, head_gate)


def attention_back_kernel(
    heads,
    dim,
    own_ref,
    other_ref,
    label_ref,
    key_label_ref,
    mask_ref,
    lse_ref,
    upstream_ref,
    query_grad_ref,
    own_grad_ref,
    other_grad_ref,
):
    rows = own_ref.shape[0]
    cols = heads * dim
    scale = dim ** (-0.5)
    labels = label_ref[...]
    same = [key_label_ref[:rows, :] == labels, key_label_ref[rows:, :] == labels]
    query_grads = []
    key_grads = [[], []]
    value_grads = [[], []]
    for head in range(heads):
        lo = head * dim
        query = own_ref[:, lo : lo + dim]
        keys = [own_ref[:, cols + lo : cols + lo + dim], other_ref[:, lo : lo + dim]]
        values = [
            own_ref[:, 2 * cols + lo : 2 * cols + lo + dim],
            other_ref[:, cols + lo : cols + lo + dim],
        ]
        upstream = (upstream_ref[:, lo : lo + dim].astype(f32) * mask_ref[:, head : head + 1]).astype(bf16)
        lse = lse_ref[head : head + 1, :] * log2e
        weights = []
        weight_grads = []
        for j in range(2):
            scores = jnp.where(same[j], dot_last(keys[j], query) * (scale * log2e), -1e30)
            weights.append(jnp.exp2(scores - lse))
            weight_grads.append(dot_last(values[j], upstream))
            value_grads[j].append(dot_plain(weights[j].astype(bf16), upstream))
        delta = jnp.sum(weights[0] * weight_grads[0], axis=0, keepdims=True)
        delta = delta + jnp.sum(weights[1] * weight_grads[1], axis=0, keepdims=True)
        query_grad = None
        for j in range(2):
            score_grad = (weights[j] * (weight_grads[j] - delta)).astype(bf16)
            key_grads[j].append(dot_plain(score_grad, query) * scale)
            term = dot_first(score_grad, keys[j])
            query_grad = term if query_grad is None else query_grad + term
        query_grads.append((query_grad * scale).astype(bf16))
    query_grad_ref[...] = jnp.concatenate(query_grads, axis=1)
    own_grad_ref[...] = jnp.concatenate(key_grads[0] + value_grads[0], axis=1)
    other_grad_ref[...] = jnp.concatenate(key_grads[1] + value_grads[1], axis=1).astype(bf16)


def attention_back(own, other, label_row, key_label_column, head_gate, lse, upstream, heads):
    rows = own.shape[0]
    cols = own.shape[1] // 3
    return pl.pallas_call(
        functools.partial(attention_back_kernel, heads, cols // heads),
        out_shape=(
            jax.ShapeDtypeStruct((rows, cols), bf16),
            jax.ShapeDtypeStruct((rows, 2 * cols), f32),
            jax.ShapeDtypeStruct((rows, 2 * cols), bf16),
        ),
        compiler_params=pltpu.CompilerParams(vmem_limit_bytes=kernel_vmem),
        cost_estimate=pl.CostEstimate(
            flops=20 * rows * rows * cols,
            bytes_accessed=2 * rows * cols * 12,
            transcendentals=2 * rows * rows * heads,
        ),
        name="attend_back",
    )(own, other, label_row, key_label_column, head_gate, lse, upstream)


def dot(left, right):
    return jnp.dot(left, right, preferred_element_type=f32)


def dot_t(left, right):
    return jnp.einsum("nf,df->nd", left, right, preferred_element_type=f32)


def outer(lefts, rights):
    left = jnp.concatenate(lefts, axis=0)
    right = jnp.concatenate(rights, axis=0)
    return jnp.einsum("nd,nf->df", left, right, preferred_element_type=f32).astype(bf16)


def on_device(
    x_in, cotangent, cond, crop_len, head_mask, skip_mask, ada_w, qkv_w, proj_w, fc1_w, fc2_w
):
    micro, local, width = x_in.shape
    row = skip_mask.shape[1]
    slots = crop_len.shape[1]
    heads = head_mask.shape[2]
    mine = local // 2
    half = mine // 2
    section = lax.axis_index("section")
    tensor_index = lax.axis_index("tensor")
    dp_index = lax.axis_index("dp")
    first_core = section == 0

    def choose(zero, one):
        return jax.tree.map(lambda a, b: jnp.where(first_core, a, b), zero, one)

    def both_blocks(own):
        other = swap_cores(own)
        return (choose(own, other), choose(other, own))

    def to_owner(zero, one):
        own = choose(zero, one)
        other = swap_cores(choose(one, zero))
        return (choose(own, other), choose(other, own))

    hc = qkv_w.shape[3]
    wqkv = both_blocks(jnp.concatenate([qkv_w[0, c] for c in range(3)], axis=1))
    wproj = both_blocks(proj_w[0])
    wup = both_blocks(fc1_w[0])
    wdown = both_blocks(fc2_w[0])

    condition = jax.nn.silu(cond.astype(f32)).astype(bf16)
    flat_condition = condition.reshape(micro * slots, width)
    mod_local = jnp.dot(flat_condition, ada_w[0], preferred_element_type=f32)
    modulation = [
        part.reshape(micro, slots, 6 * width) for part in both_blocks(gather_columns(mod_local))
    ]

    finish = jnp.cumsum(crop_len, axis=1)
    begin = finish - crop_len

    def layout(places):
        inside = (places[None, :, None] >= begin[:, None, :]) & (
            places[None, :, None] < finish[:, None, :]
        )
        flags = inside.astype(jnp.int32)
        labels = jnp.sum(flags * jnp.arange(slots, dtype=jnp.int32)[None, None, :], axis=2)
        labels = labels + (1 - jnp.sum(flags, axis=2)) * slots
        return (inside.astype(f32), labels)

    def starts(core):
        out = []
        for chunk, part in half_order():
            index = tensor_index ^ chunk if square() else chunk
            out.append(index * local + core * mine + part * half)
        return out

    def row_places(core):
        steps = jnp.arange(half, dtype=jnp.int32)
        return jnp.concatenate([start + steps for start in starts(core)])

    my_places = tensor_index * local + section * mine + jnp.arange(mine, dtype=jnp.int32)
    member, unused = layout(my_places)
    row_member, row_labels = layout(row_places(section))
    unused, other_labels = layout(row_places(1 - section))
    key_labels = jnp.concatenate([row_labels, other_labels], axis=1)
    head_gate = jnp.einsum(
        "mns,msh->mnh", row_member, head_mask.astype(f32), precision=highest
    )
    skip = jnp.concatenate(
        [lax.dynamic_slice_in_dim(skip_mask, start, half, 1) for start in starts(section)], axis=1
    ).astype(f32)

    token_mod = [
        [
            jnp.split(jnp.dot(member[i], modulation[b][i], precision=highest), 6, axis=1)
            for i in range(micro)
        ]
        for b in range(2)
    ]

    def forward(b, xs):
        outs, rms, kept = [], [], []
        for i in range(micro):
            shift_one, scale_one, gate_one, shift_two, scale_two, gate_two = token_mod[b][i]
            x = xs[i]
            normed_one, factor_one = normalize_keep(x)
            first = gather_rows((normed_one * (1.0 + scale_one) + shift_one).astype(bf16))
            qkv = dot(first, wqkv[b]).astype(bf16)
            other_kv = swap_cores(qkv[:, hc:])
            mixed, lse = attention_forward(
                qkv, other_kv, row_labels[i][:, None], key_labels[i][None, :], head_gate[i], heads
            )
            attended = scatter_rows(dot(mixed, wproj[b]).astype(bf16))
            middle = x + gate_one * attended
            normed_two, factor_two = normalize_keep(middle)
            second = gather_rows((normed_two * (1.0 + scale_two) + shift_two).astype(bf16))
            pre = dot(second, wup[b])
            hidden = (jax.nn.gelu(pre, approximate=True) * skip[i][:, None]).astype(bf16)
            feed = scatter_rows(dot(hidden, wdown[b]).astype(bf16))
            outs.append(middle + gate_two * feed)
            rms.append(
                jnp.stack(
                    [
                        jnp.sqrt(jnp.mean(attended * attended, axis=1)),
                        jnp.sqrt(jnp.mean(feed * feed, axis=1)),
                    ]
                )
            )
            kept.append((x, first, qkv, other_kv, lse.T, mixed, attended, middle, second, pre, hidden, feed))
        return (outs, jnp.stack(rms, axis=1), kept)

    def backward(b, gs, kept_all):
        grads, mods, pairs = [], [], []
        for i in range(micro):
            x, first, qkv, other_kv, lse, mixed, attended, middle, second, pre, hidden, feed = (
                kept_all[i]
            )
            shift_one, scale_one, gate_one, shift_two, scale_two, gate_two = token_mod[b][i]
            g = gs[i]
            normed_one, factor_one = normalize_keep(x)
            normed_two, factor_two = normalize_keep(middle)
            feed_rows = gather_rows((g * gate_two).astype(bf16))
            unused, activation_back = jax.vjp(
                lambda value: jax.nn.gelu(value, approximate=True) * skip[i][:, None], pre
            )
            pre_grad = activation_back(dot_t(feed_rows, wdown[b]))[0].astype(bf16)
            second_grad = scatter_rows(dot_t(pre_grad, wup[b]).astype(bf16))
            middle_grad = g + normalize_back(
                normed_two, factor_two, second_grad * (1.0 + scale_two)
            )
            attn_rows = gather_rows((middle_grad * gate_one).astype(bf16))
            mixed_grad = dot_t(attn_rows, wproj[b]).astype(bf16)
            query_grad, own_grad, other_grad = attention_back(
                qkv,
                other_kv,
                row_labels[i][None, :],
                key_labels[i][:, None],
                head_gate[i],
                lse,
                mixed_grad,
                heads,
            )
            kv_grad = (own_grad + swap_cores(other_grad).astype(f32)).astype(bf16)
            qkv_grad = jnp.concatenate([query_grad, kv_grad], axis=1)
            first_grad = scatter_rows(dot_t(qkv_grad, wqkv[b]).astype(bf16))
            grads.append(
                middle_grad
                + normalize_back(normed_one, factor_one, first_grad * (1.0 + scale_one))
            )
            token_grad = jnp.concatenate(
                [
                    first_grad,
                    first_grad * normed_one,
                    middle_grad * attended,
                    second_grad,
                    second_grad * normed_two,
                    g * feed,
                ],
                axis=1,
            )
            mods.append(jnp.einsum("ns,ne->se", member[i], token_grad, precision=highest))
            pairs.append((second, pre_grad, feed_rows, hidden, first, qkv_grad, attn_rows, mixed))
        second, pre_grad, feed_rows, hidden, first, qkv_grad, attn_rows, mixed = zip(*pairs)
        up = outer(second, pre_grad)
        down = outer(feed_rows, hidden)
        proj = outer(attn_rows, mixed)
        qkv = outer(first, qkv_grad)

        def reduced(zero, one):
            total = choose(zero, one).astype(f32) + swap_cores(choose(one, zero)).astype(f32)
            return lax.psum_scatter(total.astype(bf16), "dp", scatter_dimension=0, tiled=True)

        wide = reduced(up, down)
        narrow = reduced(qkv[:, : 2 * hc], jnp.concatenate([qkv[:, 2 * hc :], proj], axis=1))
        return (grads, jnp.concatenate(mods, axis=0), (wide, narrow))

    def my_rows(array):
        block = lax.dynamic_slice_in_dim(array, section * mine, mine, 1)
        return [block[i].astype(f32) for i in range(micro)]

    out_zero, rms_zero, kept_zero = forward(0, my_rows(x_in))
    out_one, rms_one, kept_one = forward(1, out_zero)
    back_one, mods_one, weights_one = backward(1, my_rows(cotangent), kept_one)
    back_zero, mods_zero, weights_zero = backward(0, back_one, kept_zero)

    residual = jnp.concatenate(to_owner(jnp.stack(out_zero), jnp.stack(out_one)), axis=1)
    input_grad = jnp.concatenate(
        to_owner(jnp.stack(back_zero).astype(bf16), jnp.stack(back_one).astype(bf16)), axis=1
    )
    sublayer_rms = jnp.concatenate(to_owner(rms_zero, rms_one), axis=2)

    mod_sum = choose(mods_zero, mods_one) + swap_cores(choose(mods_one, mods_zero))
    mod_all = gather_dp(scatter_columns(mod_sum))
    condition_all = gather_dp(flat_condition)
    rows_here = width // lax.axis_size("dp")
    condition_here = lax.dynamic_slice_in_dim(condition_all, dp_index * rows_here, rows_here, 2)
    ada_grad = jnp.einsum(
        "psd,pse->de", condition_here.astype(f32), mod_all, precision=highest
    )

    wide, narrow = (
        to_owner(zero, one) for zero, one in zip(weights_zero, weights_one)
    )
    up_grad = wide[0].astype(f32)
    down_grad = wide[1].astype(f32).T
    qkv_grad = jnp.stack([narrow[0][:, :hc], narrow[0][:, hc:], narrow[1][:, :hc]]).astype(f32)
    proj_grad = narrow[1][:, hc:].astype(f32).T
    return (
        residual[None],
        input_grad[None],
        sublayer_rms[None],
        ada_grad[None],
        qkv_grad[None],
        proj_grad[None],
        up_grad[None],
        down_grad[None],
    )


def solution(mesh):
    in_specs = (
        P(None, ("dp", "tensor"), None),
        P(None, ("dp", "tensor"), None),
        P(None, "dp", None),
        P(None, "dp"),
        P(None, "dp", "tensor"),
        P(None, "dp"),
        P("section", None, "tensor"),
        P("section", None, None, "tensor"),
        P("section", "tensor", None),
        P("section", None, "tensor"),
        P("section", "tensor", None),
    )
    out_specs = (
        P("section", None, ("dp", "tensor"), None),
        P("section", None, ("dp", "tensor"), None),
        P("section", None, None, ("dp", "tensor")),
        P("section", "dp", "tensor"),
        P("section", None, "dp", "tensor"),
        P("section", "tensor", "dp"),
        P("section", "dp", "tensor"),
        P("section", "tensor", "dp"),
    )
    return jax.shard_map(
        on_device, mesh=mesh, in_specs=in_specs, out_specs=out_specs, check_vma=False
    )
```

```python
import functools
import math

import jax
import jax.numpy as jnp
from jax import lax
from jax.experimental import pallas as pl
from jax.experimental.pallas import tpu as pltpu
from jax.sharding import PartitionSpec as P

highest = lax.Precision.HIGHEST
epsilon = 1e-06
f32 = jnp.float32
bf16 = jnp.bfloat16
log2e = math.log2(math.e)


def normalize_keep(value):
    centered = value - jnp.mean(value, axis=-1, keepdims=True)
    factor = lax.rsqrt(jnp.mean(centered * centered, axis=-1, keepdims=True) + epsilon)
    return (centered * factor, factor)


def normalize_back(normed, factor, upstream):
    return factor * (
        upstream
        - jnp.mean(upstream, axis=-1, keepdims=True)
        - normed * jnp.mean(upstream * normed, axis=-1, keepdims=True)
    )


def swap_cores(block):
    return lax.ppermute(block, "section", [(0, 1), (1, 0)])


def along_x(block):
    return lax.ppermute(block, "tensor", [(0, 1), (1, 0), (2, 3), (3, 2)])


def along_y(block):
    return lax.ppermute(block, "tensor", [(0, 2), (2, 0), (1, 3), (3, 1)])


def square():
    return lax.axis_size("tensor") == 4


def axes_of(stream):
    return ((along_x, 1), (along_y, 2)) if stream % 2 == 0 else ((along_y, 2), (along_x, 1))


def chunk_order(stream):
    if square():
        (unused, near), (unused, far) = axes_of(stream)
        return [0, far, near, 3]
    return range(lax.axis_size("tensor"))


def gather_start(block, stream):
    if not square():
        return (lax.all_gather(block, "tensor", axis=0, tiled=True),)
    (along, unused), (across, unused) = axes_of(stream)
    from_near = along(block)
    return (block, from_near, across(jnp.concatenate([block, from_near], axis=0)))


def assemble(pieces, target):
    if len(pieces) == 1:
        target[...] = pieces[0][...]
        return
    own, near, far = pieces
    mine = own.shape[0]
    target[:mine, :] = own[...]
    target[mine : 2 * mine, :] = far[:mine, :]
    target[2 * mine : 3 * mine, :] = near[...]
    target[3 * mine :, :] = far[mine:, :]


def partial_shapes(rows, width):
    parts = 2 if square() else 1
    return [jax.ShapeDtypeStruct((rows // parts, width), bf16)] * parts


def store_partial(refs, columns, value):
    begin = 0
    for ref in refs:
        rows = ref.shape[0]
        ref[:, columns] = value[begin : begin + rows].astype(bf16)
        begin += rows


def add_first_kernel(keep, arrived, own, send):
    mine = own.shape[0]
    own[...] = keep[:mine, :].astype(f32) + arrived[:mine, :].astype(f32)
    send[...] = (keep[mine:, :].astype(f32) + arrived[mine:, :].astype(f32)).astype(bf16)


def scatter_start(parts, stream):
    if not square():
        return (lax.psum_scatter(parts[0], "tensor", scatter_dimension=0, tiled=True),)
    (along, unused), (across, unused) = axes_of(stream)
    keep, leave = parts
    rows, width = keep.shape
    own, send = run(
        add_first_kernel,
        [
            jax.ShapeDtypeStruct((rows // 2, width), f32),
            jax.ShapeDtypeStruct((rows // 2, width), bf16),
        ],
        keep,
        along(leave),
        name="add_first",
        vmem=4,
    )
    return (own, across(send))


def scattered(pieces):
    total = pieces[0][...].astype(f32)
    for piece in pieces[1:]:
        total = total + piece[...].astype(f32)
    return total


def gather_columns(block):
    if not square():
        return lax.all_gather(block, "tensor", axis=1, tiled=True)
    from_x = along_x(block)
    from_y = along_y(block)
    pieces = jnp.stack([block, from_x, from_y, along_x(from_y)])
    here = lax.axis_index("tensor")
    return jnp.concatenate(
        [lax.dynamic_index_in_dim(pieces, here ^ j, 0, keepdims=False) for j in range(4)], axis=1
    )


def scatter_columns(partial):
    if not square():
        return lax.psum_scatter(partial, "tensor", scatter_dimension=1, tiled=True)
    here = lax.axis_index("tensor")
    columns = partial.shape[1] // 4

    def piece(distance):
        return lax.dynamic_slice_in_dim(partial, (here ^ distance) * columns, columns, 1)

    arrived = along_x(jnp.stack([piece(1), piece(3)]))
    return piece(0) + arrived[0] + along_y(piece(2) + arrived[1])


def gather_dp(block):
    size = lax.axis_size("dp")
    others = [
        lax.ppermute(block, "dp", [(i, (i + step) % size) for i in range(size)])
        for step in range(1, size)
    ]
    return jnp.stack([block] + others)


def dot_last(left, right):
    return lax.dot_general(left, right, (((1,), (1,)), ((), ())), preferred_element_type=f32)


def dot_plain(left, right):
    return lax.dot_general(left, right, (((1,), (0,)), ((), ())), preferred_element_type=f32)


def dot_first(left, right):
    return lax.dot_general(left, right, (((0,), (0,)), ((), ())), preferred_element_type=f32)


def chunks(size, most=384):
    step = most if size % most == 0 else size
    return [slice(begin, begin + step) for begin in range(0, size, step)]


def run(kernel, shapes, *arrays, name, vmem, flops=0, exps=0):
    return pl.pallas_call(
        kernel,
        out_shape=tuple(shapes),
        compiler_params=pltpu.CompilerParams(vmem_limit_bytes=vmem * 1024 * 1024),
        cost_estimate=pl.CostEstimate(
            flops=flops,
            bytes_accessed=sum(x.size * x.dtype.itemsize for x in (*arrays, *shapes)),
            transcendentals=exps,
        ),
        name=name,
    )(*arrays)


def block_mod(member, mod, index):
    width = mod.shape[1] // 6
    return dot_plain(member[...], mod[:, index * width : (index + 1) * width])


def slot_sums(member_t, value):
    high = value.astype(bf16)
    low = (value - high.astype(f32)).astype(bf16)
    return dot_plain(member_t[...], high) + dot_plain(member_t[...], low)


def root_mean(value):
    return jnp.sqrt(jnp.mean(value * value, axis=1, keepdims=True))


def first_kernel(x, member, mod, out):
    normed, unused = normalize_keep(x[...])
    out[...] = (normed * (1.0 + block_mod(member, mod, 1)) + block_mod(member, mod, 0)).astype(bf16)


def upstream_kernel(g, member, mod, out):
    out[...] = (g[...] * block_mod(member, mod, 5)).astype(bf16)


def column(row):
    return columns_of(row)[:, :1]


def columns_of(rows):
    count, size = rows.shape
    if count < 8:
        rows = jnp.concatenate([rows, jnp.zeros((8 - count, size), f32)], axis=0)
    return jnp.transpose(rows)


def rows_of(columns):
    size = columns[0].shape[0]
    blank = jnp.zeros((size, 128 - len(columns)), f32)
    return jnp.transpose(jnp.concatenate([*columns, blank], axis=1))[: len(columns), :]


def qkv_kernel(count, *refs):
    pieces, (weight, rows, query, keyvalue) = refs[:count], refs[count:]
    assemble(pieces, rows)
    size, cols = query.shape
    out = dot_last(rows[...], weight[...]).astype(bf16)
    query[...] = out[:, :cols]
    keyvalue[:, : 2 * cols] = out[:, cols:]
    keyvalue[:, 2 * cols :] = jnp.zeros((size, keyvalue.shape[1] - 2 * cols), bf16)


def attention_forward_kernel(
    heads, query_ref, own_ref, other_ref, label_ref, gate_ref, weight_ref, mixed_ref, lse_ref, *parts
):
    rows, cols = query_ref.shape
    dim = cols // heads
    scale = dim ** (-0.5)
    labels = column(label_ref[:, :rows])
    gates = columns_of(gate_ref[...])
    same = [labels == label_ref[:, :rows], labels == label_ref[:, rows:]]
    mixed = []
    totals = []
    for head in range(heads):
        part = slice(head * dim, (head + 1) * dim)
        value_part = slice(cols + head * dim, cols + (head + 1) * dim)
        query = query_ref[:, part]
        keys = [own_ref[:, part], other_ref[:, part]]
        values = [own_ref[:, value_part], other_ref[:, value_part]]
        scores = [jnp.where(same[j], dot_last(query, keys[j]), -1e30) for j in range(2)]
        peak = jnp.maximum(
            jnp.max(scores[0], axis=1, keepdims=True), jnp.max(scores[1], axis=1, keepdims=True)
        )
        expos = [jnp.exp2((scores[j] - peak) * (scale * log2e)) for j in range(2)]
        total = jnp.sum(expos[0], axis=1, keepdims=True) + jnp.sum(expos[1], axis=1, keepdims=True)
        inverse = 1.0 / total
        out = dot_plain((expos[0] * inverse).astype(bf16), values[0])
        out = out + dot_plain((expos[1] * inverse).astype(bf16), values[1])
        mixed.append((out * gates[:, head : head + 1]).astype(bf16))
        totals.append(peak * scale + jnp.log(total))
    mixed_ref[...] = jnp.concatenate(mixed, axis=1)
    lse_ref[...] = rows_of(totals)
    for columns in chunks(weight_ref.shape[1]):
        store_partial(parts, columns, dot_plain(mixed_ref[...], weight_ref[:, columns]))


def after_attention_kernel(count, *refs):
    pieces = refs[:count]
    x, member, mod, attended_out, middle_out, second_out, rms_out = refs[count:]
    attended = scattered(pieces)
    middle = x[...] + block_mod(member, mod, 2) * attended
    normed, unused = normalize_keep(middle)
    attended_out[...] = attended
    middle_out[...] = middle
    rms_out[...] = root_mean(attended)
    second_out[...] = (
        normed * (1.0 + block_mod(member, mod, 4)) + block_mod(member, mod, 3)
    ).astype(bf16)


def feed_kernel(count, *refs):
    pieces = refs[:count]
    up, down, skip, rows, hidden, slope, *parts = refs[count:]
    assemble(pieces, rows)
    inner = math.sqrt(2 / math.pi)
    half_skip = 0.5 * column(skip[...])
    for columns in chunks(up.shape[1]):
        pre = dot_plain(rows[...], up[:, columns])
        square_pre = pre * pre
        tanh = jnp.tanh(inner * pre * (1.0 + 0.044715 * square_pre))
        half_gate = half_skip * (1.0 + tanh)
        hidden[:, columns] = (pre * half_gate).astype(bf16)
        slope[:, columns] = (
            half_gate * (1.0 + pre * (1.0 - tanh) * (inner * (1.0 + 3 * 0.044715 * square_pre)))
        ).astype(bf16)
    for columns in chunks(down.shape[1]):
        store_partial(parts, columns, dot_plain(hidden[...], down[:, columns]))


def after_feed_kernel(count, last, *refs):
    pieces = refs[:count]
    middle, member, mod, *rest = refs[count:]
    feed = scattered(pieces)
    out = middle[...] + block_mod(member, mod, 5) * feed
    if last:
        feed_out, x_out, rms_out = rest
    else:
        next_mod, feed_out, x_out, rms_out, first_out = rest
        first_kernel(out, member, next_mod, first_out)
    feed_out[...] = feed
    x_out[...] = out
    rms_out[...] = root_mean(feed)


def feed_back_kernel(count, *refs):
    pieces = refs[:count]
    up, down, slope, rows, pre_grad, *parts = refs[count:]
    assemble(pieces, rows)
    for columns in chunks(up.shape[1]):
        hidden_grad = dot_last(rows[...], down[columns, :])
        pre_grad[:, columns] = (hidden_grad * slope[:, columns].astype(f32)).astype(bf16)
    for columns in chunks(up.shape[0]):
        store_partial(parts, columns, dot_last(pre_grad[...], up[columns, :]))


def after_feed_back_kernel(count, *refs):
    pieces = refs[:count]
    middle, g, attended, feed, member, member_t, mod, grad_out, attn_out, sums = refs[count:]
    width = middle.shape[1]
    second_grad = scattered(pieces)
    normed, factor = normalize_keep(middle[...])
    middle_grad = g[...] + normalize_back(
        normed, factor, second_grad * (1.0 + block_mod(member, mod, 4))
    )
    grad_out[...] = middle_grad
    attn_out[...] = (middle_grad * block_mod(member, mod, 2)).astype(bf16)
    sums[:, :width] = slot_sums(member_t, middle_grad * attended[...])
    sums[:, width : 2 * width] = slot_sums(member_t, second_grad)
    sums[:, 2 * width : 3 * width] = slot_sums(member_t, second_grad * normed)
    sums[:, 3 * width :] = slot_sums(member_t, g[...] * feed[...])


def attention_back_kernel(count, heads, *refs):
    pieces = refs[:count]
    (
        weight_ref,
        query_ref,
        own_ref,
        other_ref,
        label_ref,
        gate_ref,
        lse_ref,
        upstream_rows,
        query_grad_ref,
        own_grad_ref,
        other_grad_ref,
    ) = refs[count:]
    assemble(pieces, upstream_rows)
    rows, cols = query_ref.shape
    dim = cols // heads
    scale = dim ** (-0.5)
    labels = label_ref[:, :rows]
    gates = columns_of(gate_ref[...])
    mixed_grad = dot_last(upstream_rows[...], weight_ref[...]).astype(bf16).astype(f32)
    same = [column(labels) == labels, column(label_ref[:, rows:]) == labels]
    query_grads = []
    key_grads = [[], []]
    value_grads = [[], []]
    for head in range(heads):
        part = slice(head * dim, (head + 1) * dim)
        value_part = slice(cols + head * dim, cols + (head + 1) * dim)
        query = query_ref[:, part]
        keys = [own_ref[:, part], other_ref[:, part]]
        values = [own_ref[:, value_part], other_ref[:, value_part]]
        upstream = (mixed_grad[:, part] * gates[:, head : head + 1]).astype(bf16)
        lse = lse_ref[head : head + 1, :] * log2e
        weights = []
        weight_grads = []
        for j in range(2):
            scores = jnp.where(same[j], dot_last(keys[j], query) * (scale * log2e), -1e30)
            weights.append(jnp.exp2(scores - lse))
            weight_grads.append(dot_last(values[j], upstream))
            value_grads[j].append(dot_plain(weights[j].astype(bf16), upstream))
        delta = jnp.sum(weights[0] * weight_grads[0], axis=0, keepdims=True)
        delta = delta + jnp.sum(weights[1] * weight_grads[1], axis=0, keepdims=True)
        query_grad = None
        for j in range(2):
            score_grad = (weights[j] * (weight_grads[j] - delta)).astype(bf16)
            key_grads[j].append(dot_plain(score_grad, query) * scale)
            term = dot_first(score_grad, keys[j])
            query_grad = term if query_grad is None else query_grad + term
        query_grads.append((query_grad * scale).astype(bf16))
    query_grad_ref[...] = jnp.concatenate(query_grads, axis=1)
    own_grad_ref[...] = jnp.concatenate(key_grads[0] + value_grads[0], axis=1)
    other_grad_ref[:, : 2 * cols] = jnp.concatenate(
        key_grads[1] + value_grads[1], axis=1
    ).astype(bf16)
    other_grad_ref[:, 2 * cols :] = jnp.zeros((rows, other_grad_ref.shape[1] - 2 * cols), bf16)


def qkv_back_kernel(query_grad, own_grad, arrived, weight, grad, *parts):
    cols = own_grad.shape[1]
    total = own_grad[...] + arrived[:, :cols].astype(f32)
    grad[...] = jnp.concatenate([query_grad[...], total.astype(bf16)], axis=1)
    for columns in chunks(weight.shape[1]):
        store_partial(parts, columns, dot_plain(grad[...], weight[:, columns]))


def after_attention_back_kernel(count, last, *refs):
    pieces = refs[:count]
    x, middle_grad, member, member_t, mod, *rest = refs[count:]
    width = x.shape[1]
    first_grad = scattered(pieces)
    normed, factor = normalize_keep(x[...])
    out = middle_grad[...] + normalize_back(
        normed, factor, first_grad * (1.0 + block_mod(member, mod, 1))
    )
    if last:
        grad_out, sums = rest
    else:
        next_mod, grad_out, sums, feed_out = rest
        upstream_kernel(out, member, next_mod, feed_out)
    grad_out[...] = out
    sums[:, :width] = slot_sums(member_t, first_grad)
    sums[:, width:] = slot_sums(member_t, first_grad * normed)


def outer(lefts, rights):
    left = jnp.concatenate(lefts, axis=0)
    right = jnp.concatenate(rights, axis=0)
    return jnp.einsum("nd,nf->df", left, right, preferred_element_type=f32).astype(bf16)


def three_terms(value):
    high = lax.reduce_precision(value, 8, 7)
    rest = value - high
    low = lax.reduce_precision(rest, 8, 7)
    return jnp.concatenate([high, low, rest - low], axis=0).astype(bf16)


def on_device(
    x_in, cotangent, cond, crop_len, head_mask, skip_mask, ada_w, qkv_w, proj_w, fc1_w, fc2_w
):
    micro, local, width = x_in.shape
    row = skip_mask.shape[1]
    slots = crop_len.shape[1]
    heads = head_mask.shape[2]
    mine = local // 2
    section = lax.axis_index("section")
    tensor_index = lax.axis_index("tensor")
    dp_index = lax.axis_index("dp")
    first_core = section == 0

    def choose(zero, one):
        return jax.tree.map(lambda a, b: jnp.where(first_core, a, b), zero, one)

    def both_blocks(own):
        other = swap_cores(own)
        return (choose(own, other), choose(other, own))

    def to_owner(zero, one):
        own = choose(zero, one)
        other = swap_cores(choose(one, zero))
        return (choose(own, other), choose(other, own))

    hc = qkv_w.shape[3]
    wqkv = both_blocks(jnp.transpose(qkv_w[0], (0, 2, 1)).reshape(3 * hc, width))
    wproj = both_blocks(proj_w[0])
    wup = both_blocks(fc1_w[0])
    wdown = both_blocks(fc2_w[0])

    condition = jax.nn.silu(cond.astype(f32)).astype(bf16)
    flat_condition = condition.reshape(micro * slots, width)
    mod_local = jnp.dot(flat_condition, ada_w[0], preferred_element_type=f32)
    modulation = both_blocks(gather_columns(mod_local))
    mod = [
        [three_terms(modulation[b][i * slots : (i + 1) * slots]) for i in range(micro)]
        for b in range(2)
    ]

    finish = jnp.cumsum(crop_len, axis=1)
    begin = finish - crop_len

    def layout(places):
        inside = (places[:, :, None] >= begin[:, None, :]) & (
            places[:, :, None] < finish[:, None, :]
        )
        flags = inside.astype(jnp.int32)
        labels = jnp.sum(flags * jnp.arange(slots, dtype=jnp.int32)[None, None, :], axis=2)
        labels = labels + (1 - jnp.sum(flags, axis=2)) * slots
        return (inside.astype(f32), labels.astype(f32))

    def starts(core, stream):
        return [
            (tensor_index ^ chunk if square() else chunk) * local + core * mine
            for chunk in chunk_order(stream)
        ]

    steps = jnp.arange(mine, dtype=jnp.int32)

    def row_places(core):
        return jnp.stack(
            [
                jnp.concatenate([start + steps for start in starts(core, i)])
                for i in range(micro)
            ]
        )

    my_places = tensor_index * local + section * mine + steps
    member, unused = layout(my_places[None, :])
    row_member, row_labels = layout(row_places(section))
    unused, other_labels = layout(row_places(1 - section))
    key_labels = jnp.concatenate([row_labels, other_labels], axis=1)
    head_gate = jnp.einsum("mns,msh->mhn", row_member, head_mask.astype(f32), precision=highest)
    skip = jnp.stack(
        [
            jnp.concatenate(
                [
                    lax.dynamic_slice_in_dim(skip_mask[i], start, mine, 0)
                    for start in starts(section, i)
                ]
            )
            for i in range(micro)
        ]
    ).astype(f32)

    members = jnp.concatenate([member] * 3, axis=2).astype(bf16)
    members_t = jnp.transpose(member, (0, 2, 1)).astype(bf16)
    row_count = row_labels.shape[1]
    padded = -(-2 * hc // 128) * 128
    hidden_cols = fc1_w.shape[2]

    def shape(rows, cols, kind):
        return jax.ShapeDtypeStruct((rows, cols), kind)

    latest = [None]

    def after(arrays):
        if latest[0] is None:
            return arrays
        return lax.optimization_barrier((arrays, latest[0]))[0]

    def ends(array):
        latest[0] = array

    def stream(i, x, g, results):
        of_mine = shape(mine, width, f32)
        low_mine = shape(mine, width, bf16)
        low_rows = shape(row_count, width, bf16)
        column = shape(mine, 1, f32)
        terms = partial_shapes(row_count, width)
        tokens, tokens_t = members[i], members_t[i]
        kept = []
        (first_mine,) = run(first_kernel, [low_mine], x, tokens, mod[0][i], name="first", vmem=4)
        ends(first_mine)
        for b in range(2):
            pieces = gather_start(first_mine, i)
            yield
            pieces = after(pieces)
            first, query, keyvalue = run(
                functools.partial(qkv_kernel, len(pieces)),
                [low_rows, shape(row_count, hc, bf16), shape(row_count, padded, bf16)],
                *pieces,
                wqkv[b],
                name="qkv", vmem=8,
                flops=6 * row_count * width * hc,
            )
            other = swap_cores(keyvalue)
            mixed, lse, *parts = run(
                functools.partial(attention_forward_kernel, heads),
                [shape(row_count, hc, bf16), shape(heads, row_count, f32), *terms],
                query,
                keyvalue,
                other,
                key_labels[i][None, :],
                head_gate[i],
                wproj[b],
                name="attend", vmem=24,
                flops=8 * row_count * row_count * hc + 2 * row_count * hc * width,
                exps=2 * row_count * row_count * heads,
            )
            ends(mixed)
            pieces = scatter_start(parts, i)
            yield
            pieces = after(pieces)
            attended, middle, second_mine, rms_attended = run(
                functools.partial(after_attention_kernel, len(pieces)),
                [of_mine, of_mine, low_mine, column],
                *pieces,
                x,
                tokens,
                mod[b][i],
                name="after_attend", vmem=6,
            )
            ends(second_mine)
            pieces = gather_start(second_mine, i)
            yield
            pieces = after(pieces)
            second, hidden, slope, *parts = run(
                functools.partial(feed_kernel, len(pieces)),
                [
                    low_rows,
                    shape(row_count, hidden_cols, bf16),
                    shape(row_count, hidden_cols, bf16),
                    *terms,
                ],
                *pieces,
                wup[b],
                wdown[b],
                skip[i][None, :],
                name="feed", vmem=12,
                flops=4 * row_count * width * hidden_cols,
                exps=row_count * hidden_cols,
            )
            ends(hidden)
            pieces = scatter_start(parts, i)
            yield
            pieces = after(pieces)
            x_in_block = x
            if b == 0:
                feed, x, rms_feed, first_mine = run(
                    functools.partial(after_feed_kernel, len(pieces), False),
                    [of_mine, of_mine, column, low_mine],
                    *pieces,
                    middle,
                    tokens,
                    mod[b][i],
                    mod[1][i],
                    name="after_feed", vmem=6,
                )
            else:
                feed, x, rms_feed = run(
                    functools.partial(after_feed_kernel, len(pieces), True),
                    [of_mine, of_mine, column],
                    *pieces,
                    middle,
                    tokens,
                    mod[b][i],
                    name="after_feed", vmem=6,
                )
            ends(x)
            kept.append(
                (x_in_block, first, query, keyvalue, other, lse, mixed, attended, middle)
                + (second, hidden, slope, feed)
            )
            results["out", b, i] = x
            results["rms", b, i] = (rms_attended, rms_feed)
        (feed_mine,) = run(upstream_kernel, [low_mine], g, tokens, mod[1][i], name="upstream", vmem=4)
        ends(feed_mine)
        for b in (1, 0):
            x, first, query, keyvalue, other, lse, mixed, attended, middle = kept[b][:9]
            second, hidden, slope, feed = kept[b][9:]
            pieces = gather_start(feed_mine, i)
            yield
            pieces = after(pieces)
            feed_rows, pre_grad, *parts = run(
                functools.partial(feed_back_kernel, len(pieces)),
                [low_rows, shape(row_count, hidden_cols, bf16), *terms],
                *pieces,
                wup[b],
                wdown[b],
                slope,
                name="feed_back", vmem=12,
                flops=4 * row_count * width * hidden_cols,
            )
            ends(pre_grad)
            pieces = scatter_start(parts, i)
            yield
            pieces = after(pieces)
            middle_grad, attn_mine, sums_two = run(
                functools.partial(after_feed_back_kernel, len(pieces)),
                [of_mine, low_mine, shape(slots, 4 * width, f32)],
                *pieces,
                middle,
                g,
                attended,
                feed,
                tokens,
                tokens_t,
                mod[b][i],
                name="after_feed_back", vmem=8,
            )
            ends(attn_mine)
            pieces = gather_start(attn_mine, i)
            yield
            pieces = after(pieces)
            attn_rows, query_grad, own_grad, other_grad = run(
                functools.partial(attention_back_kernel, len(pieces), heads),
                [
                    low_rows,
                    shape(row_count, hc, bf16),
                    shape(row_count, 2 * hc, f32),
                    shape(row_count, padded, bf16),
                ],
                *pieces,
                wproj[b],
                query,
                keyvalue,
                other,
                key_labels[i][None, :],
                head_gate[i],
                lse,
                name="attend_back", vmem=32,
                flops=20 * row_count * row_count * hc + 2 * row_count * hc * width,
                exps=2 * row_count * row_count * heads,
            )
            qkv_grad, *parts = run(
                qkv_back_kernel,
                [shape(row_count, 3 * hc, bf16), *terms],
                query_grad,
                own_grad,
                swap_cores(other_grad),
                wqkv[b],
                name="qkv_back", vmem=8,
                flops=6 * row_count * width * hc,
            )
            ends(qkv_grad)
            pieces = scatter_start(parts, i)
            yield
            pieces = after(pieces)
            if b == 1:
                g, sums_one, feed_mine = run(
                    functools.partial(after_attention_back_kernel, len(pieces), False),
                    [of_mine, shape(slots, 2 * width, f32), low_mine],
                    *pieces,
                    x,
                    middle_grad,
                    tokens,
                    tokens_t,
                    mod[b][i],
                    mod[0][i],
                    name="after_attend_back", vmem=8,
                )
            else:
                g, sums_one = run(
                    functools.partial(after_attention_back_kernel, len(pieces), True),
                    [of_mine, shape(slots, 2 * width, f32)],
                    *pieces,
                    x,
                    middle_grad,
                    tokens,
                    tokens_t,
                    mod[b][i],
                    name="after_attend_back", vmem=8,
                )
            ends(g)
            results["grad", b, i] = g
            results["mod", b, i] = jnp.concatenate([sums_one, sums_two], axis=1)
            results["pairs", b, i] = (
                second, pre_grad, feed_rows, hidden, first, qkv_grad, attn_rows, mixed
            )

    def weight_sums(b):
        second, pre_grad, feed_rows, hidden, first, qkv_grad, attn_rows, mixed = zip(
            *(results["pairs", b, i] for i in range(micro))
        )
        up = outer(second, pre_grad)
        down = outer(feed_rows, hidden)
        proj = outer(attn_rows, mixed)
        qkv = outer(first, qkv_grad)

        def reduced(zero, one):
            total = choose(zero, one).astype(f32) + swap_cores(choose(one, zero)).astype(f32)
            return lax.psum_scatter(total.astype(bf16), "dp", scatter_dimension=0, tiled=True)

        wide = reduced(up, down)
        fill = ((0, 0), (0, padded - 2 * hc))
        narrow = reduced(
            jnp.pad(qkv[:, : 2 * hc], fill),
            jnp.pad(jnp.concatenate([qkv[:, 2 * hc :], proj], axis=1), fill),
        )
        return (wide, narrow)

    def my_rows(array):
        block = lax.dynamic_slice_in_dim(array, section * mine, mine, 1)
        return [block[i].astype(f32) for i in range(micro)]

    results = {}
    xs = my_rows(x_in)
    gs = my_rows(cotangent)
    running = [stream(i, xs[i], gs[i], results) for i in range(micro)]
    while running:
        running = [s for s in running if next(s, "ended") != "ended"]

    def collected(name, b):
        return [results[name, b, i] for i in range(micro)]

    out_zero, out_one = collected("out", 0), collected("out", 1)
    back_zero, back_one = collected("grad", 0), collected("grad", 1)
    rms_zero, rms_one = (
        jnp.concatenate([column for pair in collected("rms", b) for column in pair], axis=1)
        .T.reshape(micro, 2, mine)
        .transpose(1, 0, 2)
        for b in range(2)
    )
    mods_zero, mods_one = (jnp.concatenate(collected("mod", b), axis=0) for b in range(2))
    weights_one = weight_sums(1)
    weights_zero = weight_sums(0)

    residual = jnp.concatenate(to_owner(jnp.stack(out_zero), jnp.stack(out_one)), axis=1)
    input_grad = jnp.concatenate(
        to_owner(jnp.stack(back_zero).astype(bf16), jnp.stack(back_one).astype(bf16)), axis=1
    )
    sublayer_rms = jnp.concatenate(to_owner(rms_zero, rms_one), axis=2)

    mod_sum = choose(mods_zero, mods_one) + swap_cores(choose(mods_one, mods_zero))
    mod_all = gather_dp(scatter_columns(mod_sum))
    condition_all = gather_dp(flat_condition)
    rows_here = width // lax.axis_size("dp")
    condition_here = lax.dynamic_slice_in_dim(condition_all, dp_index * rows_here, rows_here, 2)
    ada_grad = jnp.einsum(
        "psd,pse->de", condition_here.astype(f32), mod_all, precision=highest
    )

    wide, narrow = (
        to_owner(zero, one) for zero, one in zip(weights_zero, weights_one)
    )
    up_grad = wide[0].astype(f32)
    down_grad = wide[1].astype(f32).T
    qkv_grad = jnp.stack([narrow[0][:, :hc], narrow[0][:, hc : 2 * hc], narrow[1][:, :hc]]).astype(f32)
    proj_grad = narrow[1][:, hc : 2 * hc].astype(f32).T
    return (
        residual[None],
        input_grad[None],
        sublayer_rms[None],
        ada_grad[None],
        qkv_grad[None],
        proj_grad[None],
        up_grad[None],
        down_grad[None],
    )


def solution(mesh):
    in_specs = (
        P(None, ("dp", "tensor"), None),
        P(None, ("dp", "tensor"), None),
        P(None, "dp", None),
        P(None, "dp"),
        P(None, "dp", "tensor"),
        P(None, "dp"),
        P("section", None, "tensor"),
        P("section", None, None, "tensor"),
        P("section", "tensor", None),
        P("section", None, "tensor"),
        P("section", "tensor", None),
    )
    out_specs = (
        P("section", None, ("dp", "tensor"), None),
        P("section", None, ("dp", "tensor"), None),
        P("section", None, None, ("dp", "tensor")),
        P("section", "dp", "tensor"),
        P("section", None, "dp", "tensor"),
        P("section", "tensor", "dp"),
        P("section", "dp", "tensor"),
        P("section", "tensor", "dp"),
    )
    return jax.shard_map(
        on_device, mesh=mesh, in_specs=in_specs, out_specs=out_specs, check_vma=False
    )
```

```python
import functools
import math

import jax
import jax.numpy as jnp
from jax import lax
from jax.experimental import pallas as pl
from jax.experimental.pallas import tpu as pltpu
from jax.sharding import PartitionSpec as P

highest = lax.Precision.HIGHEST
epsilon = 1e-06
f32 = jnp.float32
bf16 = jnp.bfloat16
log2e = math.log2(math.e)
brief = pl.CostEstimate(flops=1000000000, bytes_accessed=1, transcendentals=0)
lengthy = pl.CostEstimate(flops=12000000000, bytes_accessed=1, transcendentals=0)


def normalize_keep(value):
    centered = value - jnp.mean(value, axis=-1, keepdims=True)
    factor = lax.rsqrt(jnp.mean(centered * centered, axis=-1, keepdims=True) + epsilon)
    return (centered * factor, factor)


def normalize_back(normed, factor, upstream):
    return factor * (
        upstream
        - jnp.mean(upstream, axis=-1, keepdims=True)
        - normed * jnp.mean(upstream * normed, axis=-1, keepdims=True)
    )


def swap_cores(block):
    return lax.ppermute(block, "section", [(0, 1), (1, 0)])


def along_x(block):
    return lax.ppermute(block, "tensor", [(0, 1), (1, 0), (2, 3), (3, 2)])


def along_y(block):
    return lax.ppermute(block, "tensor", [(0, 2), (2, 0), (1, 3), (3, 1)])


def square():
    return lax.axis_size("tensor") == 4


def axes_of(stream):
    return ((along_x, 1), (along_y, 2)) if stream % 2 == 0 else ((along_y, 2), (along_x, 1))


def chunk_order(stream):
    if square():
        (unused, near), (unused, far) = axes_of(stream)
        return [0, far, near, 3]
    return range(lax.axis_size("tensor"))


def halves_kernel(near, far, near_half, far_half):
    half = near_half.shape[0]
    near_half[...] = near[:half, :]
    far_half[...] = far[half:, :]


def gather_start(block, stream):
    if not square():
        return ((lax.all_gather(block, "tensor", axis=0, tiled=True),), ())
    (along, unused), (across, unused) = axes_of(stream)
    near = along(block)
    far = across(block)
    half = block.shape[0] // 2
    near_half, far_half = run(
        halves_kernel,
        [jax.ShapeDtypeStruct((half, block.shape[1]), bf16)] * 2,
        near,
        far,
        name="halves",
        vmem=4,
    )
    return ((block, far, near, across(near_half), along(far_half)), (near_half, far_half))


def assemble(pieces, target):
    begin = 0
    for piece in pieces:
        target[begin : begin + piece.shape[0], :] = piece[...]
        begin += piece.shape[0]


def partial_shapes(rows, width):
    parts = 4 if square() else 1
    return [jax.ShapeDtypeStruct((rows // parts, width), bf16)] * parts


def store_partial(refs, columns, value):
    value = value.astype(bf16)
    if len(refs) == 1:
        refs[0][:, columns] = value
        return
    mine = refs[0].shape[0]
    half = mine // 2
    own, stay, leave_along, leave_across = refs
    own[:, columns] = value[:mine]
    stay[:half, columns] = value[mine : mine + half]
    stay[half:, columns] = value[2 * mine + half : 3 * mine]
    leave_along[:half, columns] = value[2 * mine : 2 * mine + half]
    leave_along[half:, columns] = value[3 * mine : 3 * mine + half]
    leave_across[:half, columns] = value[mine + half : 2 * mine]
    leave_across[half:, columns] = value[3 * mine + half :]


def add_kernel(left, right, out):
    out[...] = (left[...].astype(f32) + right[...].astype(f32)).astype(bf16)


def add(left, right, vmem=4):
    (total,) = run(
        add_kernel, [jax.ShapeDtypeStruct(left.shape, bf16)], left, right, name="add", vmem=vmem
    )
    return total


def add_halves_kernel(stay, first, second, far, near):
    half = far.shape[0]
    far[...] = (stay[:half, :].astype(f32) + first[half:, :].astype(f32)).astype(bf16)
    near[...] = (stay[half:, :].astype(f32) + second[half:, :].astype(f32)).astype(bf16)


def scatter_start(parts, stream):
    if not square():
        total = lax.psum_scatter(parts[0], "tensor", scatter_dimension=0, tiled=True)
        return ((total,), ())
    (along, unused), (across, unused) = axes_of(stream)
    own, stay, leave_along, leave_across = parts
    half = own.shape[0] // 2
    first, second = along(leave_along), across(leave_across)
    far, near = run(
        add_halves_kernel,
        [jax.ShapeDtypeStruct((half, own.shape[1]), bf16)] * 2,
        stay,
        first,
        second,
        name="add_halves",
        vmem=4,
    )
    return ((own, first, second, across(far), along(near)), (far, near))


def scattered(pieces):
    if len(pieces) == 1:
        return pieces[0][...].astype(f32)
    own, first, second, far, near = pieces
    half = far.shape[0]
    upper = own[:half, :].astype(f32) + first[:half, :].astype(f32) + far[...].astype(f32)
    lower = own[half:, :].astype(f32) + second[:half, :].astype(f32) + near[...].astype(f32)
    return jnp.concatenate([upper, lower], axis=0)


def gather_columns(block):
    if not square():
        return lax.all_gather(block, "tensor", axis=1, tiled=True)
    from_x = along_x(block)
    from_y = along_y(block)
    pieces = jnp.stack([block, from_x, from_y, along_x(from_y)])
    here = lax.axis_index("tensor")
    return jnp.concatenate(
        [lax.dynamic_index_in_dim(pieces, here ^ j, 0, keepdims=False) for j in range(4)], axis=1
    )


def scatter_columns(partial):
    if not square():
        return lax.psum_scatter(partial, "tensor", scatter_dimension=1, tiled=True)
    here = lax.axis_index("tensor")
    columns = partial.shape[1] // 4

    def piece(distance):
        return lax.dynamic_slice_in_dim(partial, (here ^ distance) * columns, columns, 1)

    arrived = along_x(jnp.stack([piece(1), piece(3)])).astype(f32)
    passed = along_y((piece(2).astype(f32) + arrived[1]).astype(partial.dtype))
    return (piece(0).astype(f32) + arrived[0] + passed.astype(f32)).astype(partial.dtype)


def gather_dp(block):
    size = lax.axis_size("dp")
    others = [
        lax.ppermute(block, "dp", [(i, (i + step) % size) for i in range(size)])
        for step in range(1, size)
    ]
    return jnp.stack([block] + others)


def dot_last(left, right):
    return lax.dot_general(left, right, (((1,), (1,)), ((), ())), preferred_element_type=f32)


def dot_plain(left, right):
    return lax.dot_general(left, right, (((1,), (0,)), ((), ())), preferred_element_type=f32)


def dot_first(left, right):
    return lax.dot_general(left, right, (((0,), (0,)), ((), ())), preferred_element_type=f32)


def chunks(size, most=384):
    step = most if size % most == 0 else size
    return [slice(begin, begin + step) for begin in range(0, size, step)]


matmuls = ("qkv", "attend", "feed", "feed_back", "attend_back", "qkv_back")


def run(kernel, shapes, *arrays, name, vmem):
    return pl.pallas_call(
        kernel,
        out_shape=tuple(shapes),
        compiler_params=pltpu.CompilerParams(vmem_limit_bytes=vmem * 1024 * 1024),
        cost_estimate=lengthy if name in matmuls else brief,
        name=name,
    )(*arrays)


def block_mod(member, mod, index):
    width = mod.shape[1] // 6
    return dot_plain(member[...], mod[:, index * width : (index + 1) * width])


def slot_sums(member_t, value):
    high = value.astype(bf16)
    low = (value - high.astype(f32)).astype(bf16)
    return dot_plain(member_t[...], high) + dot_plain(member_t[...], low)


def root_mean(value):
    return rows_of([jnp.sqrt(jnp.mean(value * value, axis=1, keepdims=True))])


def first_kernel(x, member, mod, out):
    normed, unused = normalize_keep(x[...])
    out[...] = (normed * (1.0 + block_mod(member, mod, 1)) + block_mod(member, mod, 0)).astype(bf16)


def upstream_kernel(g, member, mod, out):
    out[...] = (g[...] * block_mod(member, mod, 5)).astype(bf16)


def column(row):
    return columns_of(row)[:, :1]


def columns_of(rows):
    count, size = rows.shape
    if count < 8:
        rows = jnp.concatenate([rows, jnp.zeros((8 - count, size), f32)], axis=0)
    return jnp.transpose(rows)


def rows_of(columns):
    size = columns[0].shape[0]
    blank = jnp.zeros((size, 128 - len(columns)), f32)
    return jnp.transpose(jnp.concatenate([*columns, blank], axis=1))[: len(columns), :]


def qkv_first_kernel(count, *refs):
    pieces, (member, mod, weight, rows, query, keyvalue) = refs[:count], refs[count:]
    begin = 0
    for piece in pieces:
        part = slice(begin, begin + piece.shape[0])
        first_kernel(piece[...].astype(f32), member[part, :], mod, rows.at[part, :])
        begin += piece.shape[0]
    project(rows, weight, query, keyvalue)


def qkv_kernel(count, *refs):
    pieces, (weight, rows, query, keyvalue) = refs[:count], refs[count:]
    assemble(pieces, rows)
    project(rows, weight, query, keyvalue)


def project(rows, weight, query, keyvalue):
    size, cols = query.shape
    out = dot_last(rows[...], weight[...]).astype(bf16)
    query[...] = out[:, :cols]
    keyvalue[:, : 2 * cols] = out[:, cols:]
    keyvalue[:, 2 * cols :] = jnp.zeros((size, keyvalue.shape[1] - 2 * cols), bf16)


def attention_forward_kernel(
    heads, query_ref, own_ref, other_ref, label_ref, gate_ref, weight_ref, mixed_ref, lse_ref, *parts
):
    rows, cols = query_ref.shape
    dim = cols // heads
    scale = dim ** (-0.5)
    labels = column(label_ref[:, :rows])
    gates = columns_of(gate_ref[...])
    same = [labels == label_ref[:, :rows], labels == label_ref[:, rows:]]
    mixed = []
    totals = []
    for head in range(heads):
        part = slice(head * dim, (head + 1) * dim)
        value_part = slice(cols + head * dim, cols + (head + 1) * dim)
        query = query_ref[:, part]
        keys = [own_ref[:, part], other_ref[:, part]]
        values = [own_ref[:, value_part], other_ref[:, value_part]]
        scores = [jnp.where(same[j], dot_last(query, keys[j]), -1e30) for j in range(2)]
        peak = jnp.maximum(
            jnp.max(scores[0], axis=1, keepdims=True), jnp.max(scores[1], axis=1, keepdims=True)
        )
        expos = [jnp.exp2((scores[j] - peak) * (scale * log2e)) for j in range(2)]
        total = jnp.sum(expos[0], axis=1, keepdims=True) + jnp.sum(expos[1], axis=1, keepdims=True)
        inverse = 1.0 / total
        out = dot_plain((expos[0] * inverse).astype(bf16), values[0])
        out = out + dot_plain((expos[1] * inverse).astype(bf16), values[1])
        mixed.append((out * gates[:, head : head + 1]).astype(bf16))
        totals.append(peak * scale + jnp.log(total))
    mixed_ref[...] = jnp.concatenate(mixed, axis=1)
    lse_ref[...] = rows_of(totals)
    for columns in chunks(weight_ref.shape[1]):
        store_partial(parts, columns, dot_plain(mixed_ref[...], weight_ref[:, columns]))


def after_attention_kernel(count, *refs):
    pieces = refs[:count]
    x, member, mod, attended_out, middle_out, second_out, rms_out = refs[count:]
    attended = scattered(pieces)
    middle = x[...] + block_mod(member, mod, 2) * attended
    normed, unused = normalize_keep(middle)
    attended_out[...] = attended
    middle_out[...] = middle
    rms_out[...] = root_mean(attended)
    second_out[...] = (
        normed * (1.0 + block_mod(member, mod, 4)) + block_mod(member, mod, 3)
    ).astype(bf16)


def feed_kernel(count, *refs):
    pieces = refs[:count]
    up, down, skip, rows, hidden, slope, *parts = refs[count:]
    assemble(pieces, rows)
    inner = math.sqrt(2 / math.pi)
    half_skip = 0.5 * column(skip[...])
    for columns in chunks(up.shape[1]):
        pre = dot_plain(rows[...], up[:, columns])
        square_pre = pre * pre
        tanh = jnp.tanh(inner * pre * (1.0 + 0.044715 * square_pre))
        half_gate = half_skip * (1.0 + tanh)
        hidden[:, columns] = (pre * half_gate).astype(bf16)
        slope[:, columns] = (
            half_gate * (1.0 + pre * (1.0 - tanh) * (inner * (1.0 + 3 * 0.044715 * square_pre)))
        ).astype(bf16)
    for columns in chunks(down.shape[1]):
        store_partial(parts, columns, dot_plain(hidden[...], down[:, columns]))


def after_feed_kernel(count, last, *refs):
    pieces = refs[:count]
    middle, member, mod, *rest = refs[count:]
    feed = scattered(pieces)
    out = middle[...] + block_mod(member, mod, 5) * feed
    if last:
        feed_out, x_out, rms_out = rest
    else:
        next_mod, feed_out, x_out, rms_out, first_out = rest
        first_kernel(out, member, next_mod, first_out)
    feed_out[...] = feed
    x_out[...] = out
    rms_out[...] = root_mean(feed)


def feed_back_kernel(count, *refs):
    pieces = refs[:count]
    up, down, slope, rows, pre_grad, *parts = refs[count:]
    assemble(pieces, rows)
    for columns in chunks(up.shape[1]):
        hidden_grad = dot_last(rows[...], down[columns, :])
        pre_grad[:, columns] = (hidden_grad * slope[:, columns].astype(f32)).astype(bf16)
    for columns in chunks(up.shape[0]):
        store_partial(parts, columns, dot_last(pre_grad[...], up[columns, :]))


def after_feed_back_kernel(count, *refs):
    pieces = refs[:count]
    middle, g, attended, feed, member, member_t, mod, grad_out, attn_out, sums = refs[count:]
    width = middle.shape[1]
    second_grad = scattered(pieces)
    normed, factor = normalize_keep(middle[...])
    middle_grad = g[...] + normalize_back(
        normed, factor, second_grad * (1.0 + block_mod(member, mod, 4))
    )
    grad_out[...] = middle_grad
    attn_out[...] = (middle_grad * block_mod(member, mod, 2)).astype(bf16)
    sums[:, :width] = slot_sums(member_t, middle_grad * attended[...])
    sums[:, width : 2 * width] = slot_sums(member_t, second_grad)
    sums[:, 2 * width : 3 * width] = slot_sums(member_t, second_grad * normed)
    sums[:, 3 * width :] = slot_sums(member_t, g[...] * feed[...])


def attention_back_kernel(count, heads, *refs):
    pieces = refs[:count]
    (
        weight_ref,
        query_ref,
        own_ref,
        other_ref,
        label_ref,
        gate_ref,
        lse_ref,
        upstream_rows,
        query_grad_ref,
        own_grad_ref,
        other_grad_ref,
    ) = refs[count:]
    assemble(pieces, upstream_rows)
    rows, cols = query_ref.shape
    dim = cols // heads
    scale = dim ** (-0.5)
    labels = label_ref[:, :rows]
    gates = columns_of(gate_ref[...])
    mixed_grad = dot_last(upstream_rows[...], weight_ref[...]).astype(bf16).astype(f32)
    same = [column(labels) == labels, column(label_ref[:, rows:]) == labels]
    query_grads = []
    key_grads = [[], []]
    value_grads = [[], []]
    for head in range(heads):
        part = slice(head * dim, (head + 1) * dim)
        value_part = slice(cols + head * dim, cols + (head + 1) * dim)
        query = query_ref[:, part]
        keys = [own_ref[:, part], other_ref[:, part]]
        values = [own_ref[:, value_part], other_ref[:, value_part]]
        upstream = (mixed_grad[:, part] * gates[:, head : head + 1]).astype(bf16)
        lse = lse_ref[head : head + 1, :] * log2e
        weights = []
        weight_grads = []
        for j in range(2):
            scores = jnp.where(same[j], dot_last(keys[j], query) * (scale * log2e), -1e30)
            weights.append(jnp.exp2(scores - lse))
            weight_grads.append(dot_last(values[j], upstream))
            value_grads[j].append(dot_plain(weights[j].astype(bf16), upstream))
        delta = jnp.sum(weights[0] * weight_grads[0], axis=0, keepdims=True)
        delta = delta + jnp.sum(weights[1] * weight_grads[1], axis=0, keepdims=True)
        query_grad = None
        for j in range(2):
            score_grad = (weights[j] * (weight_grads[j] - delta)).astype(bf16)
            key_grads[j].append(dot_plain(score_grad, query) * scale)
            term = dot_first(score_grad, keys[j])
            query_grad = term if query_grad is None else query_grad + term
        query_grads.append((query_grad * scale).astype(bf16))
    query_grad_ref[...] = jnp.concatenate(query_grads, axis=1)
    own_grad_ref[...] = jnp.concatenate(key_grads[0] + value_grads[0], axis=1)
    other_grad_ref[:, : 2 * cols] = jnp.concatenate(
        key_grads[1] + value_grads[1], axis=1
    ).astype(bf16)
    other_grad_ref[:, 2 * cols :] = jnp.zeros((rows, other_grad_ref.shape[1] - 2 * cols), bf16)


def qkv_back_kernel(query_grad, own_grad, arrived, weight, grad, *parts):
    cols = own_grad.shape[1]
    total = own_grad[...] + arrived[:, :cols].astype(f32)
    grad[...] = jnp.concatenate([query_grad[...], total.astype(bf16)], axis=1)
    for columns in chunks(weight.shape[1]):
        store_partial(parts, columns, dot_plain(grad[...], weight[:, columns]))


def after_attention_back_kernel(count, last, *refs):
    pieces = refs[:count]
    x, middle_grad, member, member_t, mod, *rest = refs[count:]
    width = x.shape[1]
    first_grad = scattered(pieces)
    normed, factor = normalize_keep(x[...])
    out = middle_grad[...] + normalize_back(
        normed, factor, first_grad * (1.0 + block_mod(member, mod, 1))
    )
    if last:
        grad_out, sums = rest
    else:
        next_mod, grad_out, sums, feed_out = rest
        upstream_kernel(out, member, next_mod, feed_out)
    grad_out[...] = out
    sums[:, :width] = slot_sums(member_t, first_grad)
    sums[:, width:] = slot_sums(member_t, first_grad * normed)


def wide_kernel(count, flag, *refs):
    seconds, uppers, pres, hiddens = (refs[k * count : (k + 1) * count] for k in range(4))
    keep, send = refs[4 * count :]
    first_core = flag[0] == 0
    for columns in chunks(keep.shape[1]):
        up = sum(dot_first(a[...], b[:, columns]) for a, b in zip(seconds, pres)).astype(bf16)
        down = sum(dot_first(a[...], b[:, columns]) for a, b in zip(uppers, hiddens)).astype(bf16)
        keep[:, columns] = jnp.where(first_core, up, down)
        send[:, columns] = jnp.where(first_core, down, up)


def narrow_kernel(count, flag, *refs):
    firsts, uppers, grads, mixeds = (refs[k * count : (k + 1) * count] for k in range(4))
    keep, send = refs[4 * count :]
    first_core = flag[0] == 0
    qkv = sum(dot_first(a[...], b[...]) for a, b in zip(firsts, grads)).astype(bf16)
    proj = sum(dot_first(a[...], b[...]) for a, b in zip(uppers, mixeds)).astype(bf16)
    cols = proj.shape[1]
    fill = [jnp.zeros((qkv.shape[0], keep.shape[1] - 2 * cols), bf16)]
    if not fill[0].shape[1]:
        fill = []
    zero = jnp.concatenate([qkv[:, : 2 * cols], *fill], axis=1)
    one = jnp.concatenate([qkv[:, 2 * cols :], proj, *fill], axis=1)
    keep[...] = jnp.where(first_core, zero, one)
    send[...] = jnp.where(first_core, one, zero)


def weight_sums(kernel, flag, lefts, rights, width, name):
    rows, depth = lefts[0].shape
    step = chunks(depth)[0].stop

    def whole(array):
        return pl.BlockSpec(array.shape, lambda j: (0, 0))

    return pl.pallas_call(
        kernel,
        grid=(depth // step,),
        in_specs=[
            pl.BlockSpec(memory_space=pltpu.SMEM),
            *(pl.BlockSpec((rows, step), lambda j: (0, j)) for unused in lefts),
            *(whole(array) for array in rights),
        ],
        out_specs=[pl.BlockSpec((step, width), lambda j: (j, 0))] * 2,
        out_shape=[jax.ShapeDtypeStruct((depth, width), bf16)] * 2,
        compiler_params=pltpu.CompilerParams(vmem_limit_bytes=32 * 1024 * 1024),
        cost_estimate=lengthy,
        name=name,
    )(flag, *lefts, *rights)


def three_terms(value):
    high = lax.reduce_precision(value, 8, 7)
    rest = value - high
    low = lax.reduce_precision(rest, 8, 7)
    return jnp.concatenate([high, low, rest - low], axis=0).astype(bf16)


def on_device(
    x_in, cotangent, cond, crop_len, head_mask, skip_mask, ada_w, qkv_w, proj_w, fc1_w, fc2_w
):
    micro, local, width = x_in.shape
    row = skip_mask.shape[1]
    slots = crop_len.shape[1]
    heads = head_mask.shape[2]
    mine = local // 2
    section = lax.axis_index("section")
    tensor_index = lax.axis_index("tensor")
    dp_index = lax.axis_index("dp")
    first_core = section == 0

    def choose(zero, one):
        return jax.tree.map(lambda a, b: jnp.where(first_core, a, b), zero, one)

    def both_blocks(own):
        other = swap_cores(own)
        return (choose(own, other), choose(other, own))

    def to_owner(zero, one):
        own = choose(zero, one)
        other = swap_cores(choose(one, zero))
        return (choose(own, other), choose(other, own))

    hc = qkv_w.shape[3]
    wqkv = both_blocks(jnp.transpose(qkv_w[0], (0, 2, 1)).reshape(3 * hc, width))
    wproj = both_blocks(proj_w[0])
    wup = both_blocks(fc1_w[0])
    wdown = both_blocks(fc2_w[0])

    condition = jax.nn.silu(cond.astype(f32)).astype(bf16)
    flat_condition = condition.reshape(micro * slots, width)
    mod_local = jnp.dot(flat_condition, ada_w[0], preferred_element_type=f32)
    modulation = both_blocks(gather_columns(mod_local))
    mod = [
        [three_terms(modulation[b][i * slots : (i + 1) * slots]) for i in range(micro)]
        for b in range(2)
    ]

    finish = jnp.cumsum(crop_len, axis=1)
    begin = finish - crop_len

    def layout(places):
        inside = (places[:, :, None] >= begin[:, None, :]) & (
            places[:, :, None] < finish[:, None, :]
        )
        flags = inside.astype(jnp.int32)
        labels = jnp.sum(flags * jnp.arange(slots, dtype=jnp.int32)[None, None, :], axis=2)
        labels = labels + (1 - jnp.sum(flags, axis=2)) * slots
        return (inside.astype(f32), labels.astype(f32))

    def starts(core, stream):
        return [
            (tensor_index ^ chunk if square() else chunk) * local + core * mine
            for chunk in chunk_order(stream)
        ]

    steps = jnp.arange(mine, dtype=jnp.int32)

    def row_places(core):
        return jnp.stack(
            [
                jnp.concatenate([start + steps for start in starts(core, i)])
                for i in range(micro)
            ]
        )

    my_places = tensor_index * local + section * mine + steps
    member, unused = layout(my_places[None, :])
    row_member, row_labels = layout(row_places(section))
    unused, other_labels = layout(row_places(1 - section))
    key_labels = jnp.concatenate([row_labels, other_labels], axis=1)
    head_gate = jnp.einsum("mns,msh->mhn", row_member, head_mask.astype(f32), precision=highest)
    skip = jnp.stack(
        [
            jnp.concatenate(
                [
                    lax.dynamic_slice_in_dim(skip_mask[i], start, mine, 0)
                    for start in starts(section, i)
                ]
            )
            for i in range(micro)
        ]
    ).astype(f32)

    members = jnp.concatenate([member] * 3, axis=2).astype(bf16)
    row_members = jnp.concatenate([row_member] * 3, axis=2).astype(bf16)
    members_t = jnp.transpose(member, (0, 2, 1)).astype(bf16)
    row_count = row_labels.shape[1]
    padded = -(-2 * hc // 128) * 128
    hidden_cols = fc1_w.shape[2]

    def shape(rows, cols, kind):
        return jax.ShapeDtypeStruct((rows, cols), kind)

    latest = [None]
    begun = []

    def after(arrays):
        if latest[0] is None:
            return arrays
        settled = begun[-2] if len(begun) >= 2 else ()
        return lax.optimization_barrier((arrays, latest[0], settled))[0]

    def ends(array):
        latest[0] = array

    def begins(pieces, first):
        begun.append(first)
        return pieces

    def stream(i, x, g, results):
        of_mine = shape(mine, width, f32)
        low_mine = shape(mine, width, bf16)
        low_rows = shape(row_count, width, bf16)
        row_shape = shape(1, mine, f32)
        terms = partial_shapes(row_count, width)
        tokens, tokens_t = members[i], members_t[i]
        kept = []
        first_mine = x
        x = x.astype(f32)
        g = g.astype(f32)
        for b in range(2):
            pieces = begins(*gather_start(first_mine, i))
            yield
            pieces = after(pieces)
            more = [row_members[i], mod[0][i]] if b == 0 else []
            first, query, keyvalue = run(
                functools.partial(qkv_kernel if more == [] else qkv_first_kernel, len(pieces)),
                [low_rows, shape(row_count, hc, bf16), shape(row_count, padded, bf16)],
                *pieces,
                *more,
                wqkv[b],
                name="qkv", vmem=10,
            )
            ends(query)
            other = begins(swap_cores(keyvalue), ())
            yield
            other = after(other)
            mixed, lse, *parts = run(
                functools.partial(attention_forward_kernel, heads),
                [shape(row_count, hc, bf16), shape(heads, row_count, f32), *terms],
                query,
                keyvalue,
                other,
                key_labels[i][None, :],
                head_gate[i],
                wproj[b],
                name="attend", vmem=10,
            )
            ends(mixed)
            pieces = begins(*scatter_start(parts, i))
            yield
            pieces = after(pieces)
            attended, middle, second_mine, rms_attended = run(
                functools.partial(after_attention_kernel, len(pieces)),
                [of_mine, of_mine, low_mine, row_shape],
                *pieces,
                x,
                tokens,
                mod[b][i],
                name="after_attend", vmem=6,
            )
            ends(second_mine)
            pieces = begins(*gather_start(second_mine, i))
            yield
            pieces = after(pieces)
            second, hidden, slope, *parts = run(
                functools.partial(feed_kernel, len(pieces)),
                [
                    low_rows,
                    shape(row_count, hidden_cols, bf16),
                    shape(row_count, hidden_cols, bf16),
                    *terms,
                ],
                *pieces,
                wup[b],
                wdown[b],
                skip[i][None, :],
                name="feed", vmem=7,
            )
            ends(hidden)
            pieces = begins(*scatter_start(parts, i))
            yield
            pieces = after(pieces)
            x_in_block = x
            if b == 0:
                feed, x, rms_feed, first_mine = run(
                    functools.partial(after_feed_kernel, len(pieces), False),
                    [of_mine, of_mine, row_shape, low_mine],
                    *pieces,
                    middle,
                    tokens,
                    mod[b][i],
                    mod[1][i],
                    name="after_feed", vmem=6,
                )
            else:
                feed, x, rms_feed = run(
                    functools.partial(after_feed_kernel, len(pieces), True),
                    [of_mine, of_mine, row_shape],
                    *pieces,
                    middle,
                    tokens,
                    mod[b][i],
                    name="after_feed", vmem=6,
                )
            ends(x)
            kept.append(
                (x_in_block, first, query, keyvalue, other, lse, mixed, attended, middle)
                + (second, hidden, slope, feed)
            )
            results["out", b, i] = x
            results["rms", b, i] = (rms_attended, rms_feed)
        (feed_mine,) = run(upstream_kernel, [low_mine], g, tokens, mod[1][i], name="upstream", vmem=4)
        ends(feed_mine)
        for b in (1, 0):
            x, first, query, keyvalue, other, lse, mixed, attended, middle = kept[b][:9]
            second, hidden, slope, feed = kept[b][9:]
            pieces = begins(*gather_start(feed_mine, i))
            yield
            pieces = after(pieces)
            for name, array in dict(second=second, hidden=hidden, first=first, mixed=mixed).items():
                results[name, b, i] = array
            feed_rows, pre_grad, *parts = run(
                functools.partial(feed_back_kernel, len(pieces)),
                [low_rows, shape(row_count, hidden_cols, bf16), *terms],
                *pieces,
                wup[b],
                wdown[b],
                slope,
                name="feed_back", vmem=7,
            )
            ends(pre_grad)
            results["feed_rows", b, i] = feed_rows
            results["pre_grad", b, i] = pre_grad
            pieces = begins(*scatter_start(parts, i))
            yield
            pieces = after(pieces)
            middle_grad, attn_mine, sums_two = run(
                functools.partial(after_feed_back_kernel, len(pieces)),
                [of_mine, low_mine, shape(slots, 4 * width, f32)],
                *pieces,
                middle,
                g,
                attended,
                feed,
                tokens,
                tokens_t,
                mod[b][i],
                name="after_feed_back", vmem=8,
            )
            ends(attn_mine)
            pieces = begins(*gather_start(attn_mine, i))
            yield
            pieces = after(pieces)
            attn_rows, query_grad, own_grad, other_grad = run(
                functools.partial(attention_back_kernel, len(pieces), heads),
                [
                    low_rows,
                    shape(row_count, hc, bf16),
                    shape(row_count, 2 * hc, f32),
                    shape(row_count, padded, bf16),
                ],
                *pieces,
                wproj[b],
                query,
                keyvalue,
                other,
                key_labels[i][None, :],
                head_gate[i],
                lse,
                name="attend_back", vmem=14,
            )
            ends(query_grad)
            arrived = begins(swap_cores(other_grad), ())
            yield
            arrived = after(arrived)
            qkv_grad, *parts = run(
                qkv_back_kernel,
                [shape(row_count, 3 * hc, bf16), *terms],
                query_grad,
                own_grad,
                arrived,
                wqkv[b],
                name="qkv_back", vmem=5,
            )
            ends(qkv_grad)
            results["attn_rows", b, i] = attn_rows
            results["qkv_grad", b, i] = qkv_grad
            pieces = begins(*scatter_start(parts, i))
            yield
            pieces = after(pieces)
            if b == 1:
                g, sums_one, feed_mine = run(
                    functools.partial(after_attention_back_kernel, len(pieces), False),
                    [of_mine, shape(slots, 2 * width, f32), low_mine],
                    *pieces,
                    x,
                    middle_grad,
                    tokens,
                    tokens_t,
                    mod[b][i],
                    mod[0][i],
                    name="after_attend_back", vmem=8,
                )
            else:
                g, sums_one = run(
                    functools.partial(after_attention_back_kernel, len(pieces), True),
                    [of_mine, shape(slots, 2 * width, f32)],
                    *pieces,
                    x,
                    middle_grad,
                    tokens,
                    tokens_t,
                    mod[b][i],
                    name="after_attend_back", vmem=8,
                )
            ends(g)
            results["grad", b, i] = g
            results["mod", b, i] = jnp.concatenate([sums_one, sums_two], axis=1)

    flag = section.astype(jnp.int32)[None]

    def summed(kernel, name, b, lefts, rights, cols):
        lefts = [array for group in lefts for array in collected(group, b)]
        rights = [array for group in rights for array in collected(group, b)]
        lefts, rights = after((lefts, rights))
        keep, send = weight_sums(
            functools.partial(kernel, micro), flag, lefts, rights, cols, name
        )
        ends(keep)
        results[name, b] = (keep, swap_cores(send))

    def reduced(name, b):
        if (name, b) == ("narrow", 0):
            total = add(*results[name, b], vmem=12)
        else:
            total = add(*after(results[name, b]), vmem=12)
            ends(total)
        results[name, b] = lax.psum_scatter(total, "dp", scatter_dimension=0, tiled=True)

    def wide(b):
        summed(
            wide_kernel, "wide", b, ("second", "feed_rows"), ("pre_grad", "hidden"), hidden_cols
        )

    def narrow(b):
        summed(
            narrow_kernel, "narrow", b, ("first", "attn_rows"), ("qkv_grad", "mixed"), padded
        )

    def my_rows(array):
        block = lax.dynamic_slice_in_dim(array, section * mine, mine, 1)
        return [block[i] for i in range(micro)]

    results = {}

    def collected(name, b):
        return [results[name, b, i] for i in range(micro)]

    xs = my_rows(x_in)
    gs = my_rows(cotangent)
    running = [stream(i, xs[i], gs[i], results) for i in range(micro)]
    extra = {12: (wide, 1), 15: (narrow, 1), 17: (wide, 0)}
    ready = {13: ("wide", 1), 16: ("narrow", 1), 18: ("wide", 0)}
    settled = {16: ("wide", 1), 19: ("narrow", 1)}
    for step in range(21):
        for i, one in enumerate(running):
            if step == 20 and i == 0:
                narrow(0)
            if step < 21:
                next(one, None)
            behind = step
            if i == 0 and behind in ready:
                reduced(*ready[behind])
            if i == micro - 1 and behind in extra:
                work, b = extra[behind]
                work(b)
            if i == 0 and behind in settled:
                ends((latest[0], results[settled[behind]]))

    reduced("narrow", 0)
    out_zero, out_one = collected("out", 0), collected("out", 1)
    back_zero, back_one = collected("grad", 0), collected("grad", 1)
    rms_zero, rms_one = (
        jnp.stack(
            [jnp.concatenate([pair[k] for pair in collected("rms", b)]) for k in range(2)]
        )
        for b in range(2)
    )
    mods_zero, mods_one = (jnp.concatenate(collected("mod", b), axis=0) for b in range(2))
    weights_zero, weights_one = (
        (results["wide", b], results["narrow", b]) for b in range(2)
    )

    residual = jnp.concatenate(to_owner(jnp.stack(out_zero), jnp.stack(out_one)), axis=1)
    input_grad = jnp.concatenate(
        to_owner(jnp.stack(back_zero).astype(bf16), jnp.stack(back_one).astype(bf16)), axis=1
    )
    sublayer_rms = jnp.concatenate(to_owner(rms_zero, rms_one), axis=2)

    mod_sum = choose(mods_zero, mods_one) + swap_cores(choose(mods_one, mods_zero))
    mod_here = scatter_columns(mod_sum.astype(bf16))
    mod_here = lax.optimization_barrier((mod_here, results["wide", 0]))[0]
    mod_all = gather_dp(mod_here)
    condition_all = gather_dp(flat_condition)
    rows_here = width // lax.axis_size("dp")
    condition_here = lax.dynamic_slice_in_dim(condition_all, dp_index * rows_here, rows_here, 2)
    ada_grad = jnp.einsum(
        "psd,pse->de", condition_here, mod_all, preferred_element_type=f32
    )

    wide, narrow = (
        to_owner(zero, one) for zero, one in zip(weights_zero, weights_one)
    )
    up_grad = wide[0].astype(f32)
    down_grad = wide[1].astype(f32).T
    qkv_grad = jnp.stack([narrow[0][:, :hc], narrow[0][:, hc : 2 * hc], narrow[1][:, :hc]]).astype(f32)
    proj_grad = narrow[1][:, hc : 2 * hc].astype(f32).T
    return (
        residual[None],
        input_grad[None],
        sublayer_rms[None],
        ada_grad[None],
        qkv_grad[None],
        proj_grad[None],
        up_grad[None],
        down_grad[None],
    )


def solution(mesh):
    in_specs = (
        P(None, ("dp", "tensor"), None),
        P(None, ("dp", "tensor"), None),
        P(None, "dp", None),
        P(None, "dp"),
        P(None, "dp", "tensor"),
        P(None, "dp"),
        P("section", None, "tensor"),
        P("section", None, None, "tensor"),
        P("section", "tensor", None),
        P("section", None, "tensor"),
        P("section", "tensor", None),
    )
    out_specs = (
        P("section", None, ("dp", "tensor"), None),
        P("section", None, ("dp", "tensor"), None),
        P("section", None, None, ("dp", "tensor")),
        P("section", "dp", "tensor"),
        P("section", None, "dp", "tensor"),
        P("section", "tensor", "dp"),
        P("section", "dp", "tensor"),
        P("section", "tensor", "dp"),
    )
    return jax.shard_map(
        on_device, mesh=mesh, in_specs=in_specs, out_specs=out_specs, check_vma=False
    )
```

```python
import functools
import math

import jax
import jax.numpy as jnp
from jax import lax
from jax.experimental import pallas as pl
from jax.experimental.pallas import tpu as pltpu
from jax.sharding import PartitionSpec as P

highest = lax.Precision.HIGHEST
epsilon = 1e-06
f32 = jnp.float32
bf16 = jnp.bfloat16
log2e = math.log2(math.e)
brief = pl.CostEstimate(flops=1000000000, bytes_accessed=1, transcendentals=0)
lengthy = pl.CostEstimate(flops=9000000000, bytes_accessed=1, transcendentals=0)


def normalize_keep(value):
    centered = value - jnp.mean(value, axis=-1, keepdims=True)
    factor = lax.rsqrt(jnp.mean(centered * centered, axis=-1, keepdims=True) + epsilon)
    return (centered * factor, factor)


def normalize_back(normed, factor, upstream):
    return factor * (
        upstream
        - jnp.mean(upstream, axis=-1, keepdims=True)
        - normed * jnp.mean(upstream * normed, axis=-1, keepdims=True)
    )


def swap_cores(block):
    return lax.ppermute(block, "section", [(0, 1), (1, 0)])


def along_x(block):
    return lax.ppermute(block, "tensor", [(0, 1), (1, 0), (2, 3), (3, 2)])


def along_y(block):
    return lax.ppermute(block, "tensor", [(0, 2), (2, 0), (1, 3), (3, 1)])


def square():
    return lax.axis_size("tensor") == 4


def axes_of(stream):
    return ((along_x, 1), (along_y, 2)) if stream % 2 == 0 else ((along_y, 2), (along_x, 1))


def chunk_order(stream):
    if square():
        (unused, near), (unused, far) = axes_of(stream)
        return [0, far, near, 3]
    return range(lax.axis_size("tensor"))


def halves_kernel(near, far, near_half, far_half):
    half = near_half.shape[0]
    near_half[...] = near[:half, :]
    far_half[...] = far[half:, :]


def gather_start(block, stream):
    if not square():
        return ((lax.all_gather(block, "tensor", axis=0, tiled=True),), ())
    (along, unused), (across, unused) = axes_of(stream)
    near = along(block)
    far = across(block)
    half = block.shape[0] // 2
    near_half, far_half = run(
        halves_kernel,
        [jax.ShapeDtypeStruct((half, block.shape[1]), bf16)] * 2,
        near,
        far,
        name="halves",
        vmem=4,
    )
    return ((block, far, near, across(near_half), along(far_half)), (near_half, far_half))


def assemble(pieces, target):
    begin = 0
    for piece in pieces:
        target[begin : begin + piece.shape[0], :] = piece[...]
        begin += piece.shape[0]


def partial_shapes(rows, width):
    parts = 4 if square() else 1
    return [jax.ShapeDtypeStruct((rows // parts, width), bf16)] * parts


def store_partial(refs, columns, value):
    value = value.astype(bf16)
    if len(refs) == 1:
        refs[0][:, columns] = value
        return
    mine = refs[0].shape[0]
    half = mine // 2
    own, stay, leave_along, leave_across = refs
    own[:, columns] = value[:mine]
    stay[:half, columns] = value[mine : mine + half]
    stay[half:, columns] = value[2 * mine + half : 3 * mine]
    leave_along[:half, columns] = value[2 * mine : 2 * mine + half]
    leave_along[half:, columns] = value[3 * mine : 3 * mine + half]
    leave_across[:half, columns] = value[mine + half : 2 * mine]
    leave_across[half:, columns] = value[3 * mine + half :]


def add_kernel(left, right, out):
    out[...] = (left[...].astype(f32) + right[...].astype(f32)).astype(bf16)


def add(left, right, vmem=4):
    (total,) = run(
        add_kernel, [jax.ShapeDtypeStruct(left.shape, bf16)], left, right, name="add", vmem=vmem
    )
    return total


def add_halves_kernel(stay, first, second, far, near):
    half = far.shape[0]
    far[...] = (stay[:half, :].astype(f32) + first[half:, :].astype(f32)).astype(bf16)
    near[...] = (stay[half:, :].astype(f32) + second[half:, :].astype(f32)).astype(bf16)


def scatter_start(parts, stream):
    if not square():
        total = lax.psum_scatter(parts[0], "tensor", scatter_dimension=0, tiled=True)
        return ((total,), ())
    (along, unused), (across, unused) = axes_of(stream)
    own, stay, leave_along, leave_across = parts
    half = own.shape[0] // 2
    first, second = along(leave_along), across(leave_across)
    far, near = run(
        add_halves_kernel,
        [jax.ShapeDtypeStruct((half, own.shape[1]), bf16)] * 2,
        stay,
        first,
        second,
        name="add_halves",
        vmem=4,
    )
    return ((own, first, second, across(far), along(near)), (far, near))


def scattered(pieces):
    if len(pieces) == 1:
        return pieces[0][...].astype(f32)
    own, first, second, far, near = pieces
    half = far.shape[0]
    upper = own[:half, :].astype(f32) + first[:half, :].astype(f32) + far[...].astype(f32)
    lower = own[half:, :].astype(f32) + second[:half, :].astype(f32) + near[...].astype(f32)
    return jnp.concatenate([upper, lower], axis=0)


def gather_columns(block):
    if not square():
        return lax.all_gather(block, "tensor", axis=1, tiled=True)
    from_x = along_x(block)
    from_y = along_y(block)
    pieces = jnp.stack([block, from_x, from_y, along_x(from_y)])
    here = lax.axis_index("tensor")
    return jnp.concatenate(
        [lax.dynamic_index_in_dim(pieces, here ^ j, 0, keepdims=False) for j in range(4)], axis=1
    )


def scatter_columns(partial):
    if not square():
        return lax.psum_scatter(partial, "tensor", scatter_dimension=1, tiled=True)
    here = lax.axis_index("tensor")
    columns = partial.shape[1] // 4

    def piece(distance):
        return lax.dynamic_slice_in_dim(partial, (here ^ distance) * columns, columns, 1)

    arrived = along_x(jnp.stack([piece(1), piece(3)])).astype(f32)
    passed = along_y((piece(2).astype(f32) + arrived[1]).astype(partial.dtype))
    return (piece(0).astype(f32) + arrived[0] + passed.astype(f32)).astype(partial.dtype)


def gather_dp(block):
    size = lax.axis_size("dp")
    others = [
        lax.ppermute(block, "dp", [(i, (i + step) % size) for i in range(size)])
        for step in range(1, size)
    ]
    return jnp.stack([block] + others)


def dot_last(left, right):
    return lax.dot_general(left, right, (((1,), (1,)), ((), ())), preferred_element_type=f32)


def dot_plain(left, right):
    return lax.dot_general(left, right, (((1,), (0,)), ((), ())), preferred_element_type=f32)


def dot_first(left, right):
    return lax.dot_general(left, right, (((0,), (0,)), ((), ())), preferred_element_type=f32)


def chunks(size, most=384):
    step = most if size % most == 0 else size
    return [slice(begin, begin + step) for begin in range(0, size, step)]


matmuls = ("qkv", "attend", "feed", "feed_back", "attend_back", "qkv_back")


def run(kernel, shapes, *arrays, name, vmem):
    return pl.pallas_call(
        kernel,
        out_shape=tuple(shapes),
        compiler_params=pltpu.CompilerParams(vmem_limit_bytes=vmem * 1024 * 1024),
        cost_estimate=lengthy if name in matmuls else brief,
        name=name,
    )(*arrays)


def block_mod(member, mod, index):
    width = mod.shape[1] // 6
    return dot_plain(member[...], mod[:, index * width : (index + 1) * width])


def slot_sums(member_t, value):
    high = value.astype(bf16)
    low = (value - high.astype(f32)).astype(bf16)
    return dot_plain(member_t[...], high) + dot_plain(member_t[...], low)


def root_mean(value):
    return rows_of([jnp.sqrt(jnp.mean(value * value, axis=1, keepdims=True))])


def first_kernel(x, member, mod, out):
    normed, unused = normalize_keep(x[...])
    out[...] = (normed * (1.0 + block_mod(member, mod, 1)) + block_mod(member, mod, 0)).astype(bf16)


def upstream_kernel(g, member, mod, out):
    out[...] = (g[...] * block_mod(member, mod, 5)).astype(bf16)


def column(row):
    return columns_of(row)[:, :1]


def columns_of(rows):
    count, size = rows.shape
    if count < 8:
        rows = jnp.concatenate([rows, jnp.zeros((8 - count, size), f32)], axis=0)
    return jnp.transpose(rows)


def rows_of(columns):
    size = columns[0].shape[0]
    blank = jnp.zeros((size, 128 - len(columns)), f32)
    return jnp.transpose(jnp.concatenate([*columns, blank], axis=1))[: len(columns), :]


def qkv_first_kernel(count, *refs):
    pieces, (member, mod, weight, rows, query, keyvalue) = refs[:count], refs[count:]
    begin = 0
    for piece in pieces:
        part = slice(begin, begin + piece.shape[0])
        first_kernel(piece[...].astype(f32), member[part, :], mod, rows.at[part, :])
        begin += piece.shape[0]
    project(rows, weight, query, keyvalue)


def qkv_kernel(count, *refs):
    pieces, (weight, rows, query, keyvalue) = refs[:count], refs[count:]
    assemble(pieces, rows)
    project(rows, weight, query, keyvalue)


def project(rows, weight, query, keyvalue):
    size, cols = query.shape
    out = dot_last(rows[...], weight[...]).astype(bf16)
    query[...] = out[:, :cols]
    keyvalue[:, : 2 * cols] = out[:, cols:]
    keyvalue[:, 2 * cols :] = jnp.zeros((size, keyvalue.shape[1] - 2 * cols), bf16)


def attention_forward_kernel(
    heads, query_ref, own_ref, other_ref, label_ref, gate_ref, weight_ref, mixed_ref, lse_ref, *parts
):
    rows, cols = query_ref.shape
    dim = cols // heads
    scale = dim ** (-0.5)
    labels = column(label_ref[:, :rows])
    gates = columns_of(gate_ref[...])
    same = [labels == label_ref[:, :rows], labels == label_ref[:, rows:]]
    mixed = []
    totals = []
    for head in range(heads):
        part = slice(head * dim, (head + 1) * dim)
        value_part = slice(cols + head * dim, cols + (head + 1) * dim)
        query = query_ref[:, part]
        keys = [own_ref[:, part], other_ref[:, part]]
        values = [own_ref[:, value_part], other_ref[:, value_part]]
        scores = [jnp.where(same[j], dot_last(query, keys[j]), -1e30) for j in range(2)]
        peak = jnp.maximum(
            jnp.max(scores[0], axis=1, keepdims=True), jnp.max(scores[1], axis=1, keepdims=True)
        )
        expos = [jnp.exp2((scores[j] - peak) * (scale * log2e)) for j in range(2)]
        total = jnp.sum(expos[0], axis=1, keepdims=True) + jnp.sum(expos[1], axis=1, keepdims=True)
        inverse = 1.0 / total
        out = dot_plain((expos[0] * inverse).astype(bf16), values[0])
        out = out + dot_plain((expos[1] * inverse).astype(bf16), values[1])
        mixed.append((out * gates[:, head : head + 1]).astype(bf16))
        totals.append(peak * scale + jnp.log(total))
    mixed_ref[...] = jnp.concatenate(mixed, axis=1)
    lse_ref[...] = rows_of(totals)
    for columns in chunks(weight_ref.shape[1]):
        store_partial(parts, columns, dot_plain(mixed_ref[...], weight_ref[:, columns]))


def after_attention_kernel(count, *refs):
    pieces = refs[:count]
    x, member, mod, attended_out, middle_out, second_out, rms_out = refs[count:]
    attended = scattered(pieces)
    middle = x[...] + block_mod(member, mod, 2) * attended
    normed, unused = normalize_keep(middle)
    attended_out[...] = attended
    middle_out[...] = middle
    rms_out[...] = root_mean(attended)
    second_out[...] = (
        normed * (1.0 + block_mod(member, mod, 4)) + block_mod(member, mod, 3)
    ).astype(bf16)


def feed_kernel(count, *refs):
    pieces = refs[:count]
    up, down, skip, rows, hidden, slope, *parts = refs[count:]
    assemble(pieces, rows)
    inner = math.sqrt(2 / math.pi)
    half_skip = 0.5 * column(skip[...])
    for columns in chunks(up.shape[1]):
        pre = dot_plain(rows[...], up[:, columns])
        square_pre = pre * pre
        tanh = jnp.tanh(inner * pre * (1.0 + 0.044715 * square_pre))
        half_gate = half_skip * (1.0 + tanh)
        hidden[:, columns] = (pre * half_gate).astype(bf16)
        slope[:, columns] = (
            half_gate * (1.0 + pre * (1.0 - tanh) * (inner * (1.0 + 3 * 0.044715 * square_pre)))
        ).astype(bf16)
    for columns in chunks(down.shape[1]):
        store_partial(parts, columns, dot_plain(hidden[...], down[:, columns]))


def after_feed_kernel(count, last, *refs):
    pieces = refs[:count]
    middle, member, mod, *rest = refs[count:]
    feed = scattered(pieces)
    out = middle[...] + block_mod(member, mod, 5) * feed
    if last:
        feed_out, x_out, rms_out = rest
    else:
        next_mod, feed_out, x_out, rms_out, first_out = rest
        first_kernel(out, member, next_mod, first_out)
    feed_out[...] = feed
    x_out[...] = out
    rms_out[...] = root_mean(feed)


def feed_back_kernel(count, *refs):
    pieces = refs[:count]
    up, down, slope, rows, pre_grad, *parts = refs[count:]
    assemble(pieces, rows)
    for columns in chunks(up.shape[1]):
        hidden_grad = dot_last(rows[...], down[columns, :])
        pre_grad[:, columns] = (hidden_grad * slope[:, columns].astype(f32)).astype(bf16)
    for columns in chunks(up.shape[0]):
        store_partial(parts, columns, dot_last(pre_grad[...], up[columns, :]))


def after_feed_back_kernel(count, *refs):
    pieces = refs[:count]
    middle, g, attended, feed, member, member_t, mod, grad_out, attn_out, sums = refs[count:]
    width = middle.shape[1]
    second_grad = scattered(pieces)
    normed, factor = normalize_keep(middle[...])
    middle_grad = g[...] + normalize_back(
        normed, factor, second_grad * (1.0 + block_mod(member, mod, 4))
    )
    grad_out[...] = middle_grad
    attn_out[...] = (middle_grad * block_mod(member, mod, 2)).astype(bf16)
    sums[:, :width] = slot_sums(member_t, middle_grad * attended[...])
    sums[:, width : 2 * width] = slot_sums(member_t, second_grad)
    sums[:, 2 * width : 3 * width] = slot_sums(member_t, second_grad * normed)
    sums[:, 3 * width :] = slot_sums(member_t, g[...] * feed[...])


def attention_back_kernel(count, heads, *refs):
    pieces = refs[:count]
    (
        weight_ref,
        query_ref,
        own_ref,
        other_ref,
        label_ref,
        gate_ref,
        lse_ref,
        upstream_rows,
        query_grad_ref,
        own_grad_ref,
        other_grad_ref,
    ) = refs[count:]
    assemble(pieces, upstream_rows)
    rows, cols = query_ref.shape
    dim = cols // heads
    scale = dim ** (-0.5)
    labels = label_ref[:, :rows]
    gates = columns_of(gate_ref[...])
    mixed_grad = dot_last(upstream_rows[...], weight_ref[...]).astype(bf16).astype(f32)
    same = [column(labels) == labels, column(label_ref[:, rows:]) == labels]
    query_grads = []
    key_grads = [[], []]
    value_grads = [[], []]
    for head in range(heads):
        part = slice(head * dim, (head + 1) * dim)
        value_part = slice(cols + head * dim, cols + (head + 1) * dim)
        query = query_ref[:, part]
        keys = [own_ref[:, part], other_ref[:, part]]
        values = [own_ref[:, value_part], other_ref[:, value_part]]
        upstream = (mixed_grad[:, part] * gates[:, head : head + 1]).astype(bf16)
        lse = lse_ref[head : head + 1, :] * log2e
        weights = []
        weight_grads = []
        for j in range(2):
            scores = jnp.where(same[j], dot_last(keys[j], query) * (scale * log2e), -1e30)
            weights.append(jnp.exp2(scores - lse))
            weight_grads.append(dot_last(values[j], upstream))
            value_grads[j].append(dot_plain(weights[j].astype(bf16), upstream))
        delta = jnp.sum(weights[0] * weight_grads[0], axis=0, keepdims=True)
        delta = delta + jnp.sum(weights[1] * weight_grads[1], axis=0, keepdims=True)
        query_grad = None
        for j in range(2):
            score_grad = (weights[j] * (weight_grads[j] - delta)).astype(bf16)
            key_grads[j].append(dot_plain(score_grad, query) * scale)
            term = dot_first(score_grad, keys[j])
            query_grad = term if query_grad is None else query_grad + term
        query_grads.append((query_grad * scale).astype(bf16))
    query_grad_ref[...] = jnp.concatenate(query_grads, axis=1)
    own_grad_ref[...] = jnp.concatenate(key_grads[0] + value_grads[0], axis=1)
    other_grad_ref[:, : 2 * cols] = jnp.concatenate(
        key_grads[1] + value_grads[1], axis=1
    ).astype(bf16)
    other_grad_ref[:, 2 * cols :] = jnp.zeros((rows, other_grad_ref.shape[1] - 2 * cols), bf16)


def qkv_back_kernel(query_grad, own_grad, arrived, weight, grad, *parts):
    cols = own_grad.shape[1]
    total = own_grad[...] + arrived[:, :cols].astype(f32)
    grad[...] = jnp.concatenate([query_grad[...], total.astype(bf16)], axis=1)
    for columns in chunks(weight.shape[1]):
        store_partial(parts, columns, dot_plain(grad[...], weight[:, columns]))


def after_attention_back_kernel(count, last, *refs):
    pieces = refs[:count]
    x, middle_grad, member, member_t, mod, *rest = refs[count:]
    width = x.shape[1]
    first_grad = scattered(pieces)
    normed, factor = normalize_keep(x[...])
    out = middle_grad[...] + normalize_back(
        normed, factor, first_grad * (1.0 + block_mod(member, mod, 1))
    )
    if last:
        grad_out, sums = rest
    else:
        next_mod, grad_out, sums, feed_out = rest
        upstream_kernel(out, member, next_mod, feed_out)
    grad_out[...] = out
    sums[:, :width] = slot_sums(member_t, first_grad)
    sums[:, width:] = slot_sums(member_t, first_grad * normed)


def wide_kernel(count, flag, *refs):
    seconds, uppers, pres, hiddens = (refs[k * count : (k + 1) * count] for k in range(4))
    keep, send = refs[4 * count :]
    first_core = flag[0] == 0
    for columns in chunks(keep.shape[1]):
        up = sum(dot_first(a[...], b[:, columns]) for a, b in zip(seconds, pres)).astype(bf16)
        down = sum(dot_first(a[...], b[:, columns]) for a, b in zip(uppers, hiddens)).astype(bf16)
        keep[:, columns] = jnp.where(first_core, up, down)
        send[:, columns] = jnp.where(first_core, down, up)


def narrow_kernel(count, flag, *refs):
    firsts, uppers, grads, mixeds = (refs[k * count : (k + 1) * count] for k in range(4))
    keep, send = refs[4 * count :]
    first_core = flag[0] == 0
    qkv = sum(dot_first(a[...], b[...]) for a, b in zip(firsts, grads)).astype(bf16)
    proj = sum(dot_first(a[...], b[...]) for a, b in zip(uppers, mixeds)).astype(bf16)
    cols = proj.shape[1]
    fill = [jnp.zeros((qkv.shape[0], keep.shape[1] - 2 * cols), bf16)]
    if not fill[0].shape[1]:
        fill = []
    zero = jnp.concatenate([qkv[:, : 2 * cols], *fill], axis=1)
    one = jnp.concatenate([qkv[:, 2 * cols :], proj, *fill], axis=1)
    keep[...] = jnp.where(first_core, zero, one)
    send[...] = jnp.where(first_core, one, zero)


def weight_sums(kernel, flag, lefts, rights, width, name):
    rows, depth = lefts[0].shape
    step = chunks(depth)[0].stop

    def whole(array):
        return pl.BlockSpec(array.shape, lambda j: (0, 0))

    return pl.pallas_call(
        kernel,
        grid=(depth // step,),
        in_specs=[
            pl.BlockSpec(memory_space=pltpu.SMEM),
            *(pl.BlockSpec((rows, step), lambda j: (0, j)) for unused in lefts),
            *(whole(array) for array in rights),
        ],
        out_specs=[pl.BlockSpec((step, width), lambda j: (j, 0))] * 2,
        out_shape=[jax.ShapeDtypeStruct((depth, width), bf16)] * 2,
        compiler_params=pltpu.CompilerParams(vmem_limit_bytes=32 * 1024 * 1024),
        cost_estimate=lengthy,
        name=name,
    )(flag, *lefts, *rights)


def three_terms(value):
    high = lax.reduce_precision(value, 8, 7)
    rest = value - high
    low = lax.reduce_precision(rest, 8, 7)
    return jnp.concatenate([high, low, rest - low], axis=0).astype(bf16)


def on_device(
    x_in, cotangent, cond, crop_len, head_mask, skip_mask, ada_w, qkv_w, proj_w, fc1_w, fc2_w
):
    micro, local, width = x_in.shape
    row = skip_mask.shape[1]
    slots = crop_len.shape[1]
    heads = head_mask.shape[2]
    mine = local // 2
    section = lax.axis_index("section")
    tensor_index = lax.axis_index("tensor")
    dp_index = lax.axis_index("dp")
    first_core = section == 0

    def choose(zero, one):
        return jax.tree.map(lambda a, b: jnp.where(first_core, a, b), zero, one)

    def both_blocks(own):
        other = swap_cores(own)
        return (choose(own, other), choose(other, own))

    def to_owner(zero, one):
        own = choose(zero, one)
        other = swap_cores(choose(one, zero))
        return (choose(own, other), choose(other, own))

    hc = qkv_w.shape[3]
    wqkv = both_blocks(jnp.transpose(qkv_w[0], (0, 2, 1)).reshape(3 * hc, width))
    wproj = both_blocks(proj_w[0])
    wup = both_blocks(fc1_w[0])
    wdown = both_blocks(fc2_w[0])

    condition = jax.nn.silu(cond.astype(f32)).astype(bf16)
    flat_condition = condition.reshape(micro * slots, width)
    mod_local = jnp.dot(flat_condition, ada_w[0], preferred_element_type=f32)
    modulation = both_blocks(gather_columns(mod_local))
    mod = [
        [three_terms(modulation[b][i * slots : (i + 1) * slots]) for i in range(micro)]
        for b in range(2)
    ]

    finish = jnp.cumsum(crop_len, axis=1)
    begin = finish - crop_len

    def layout(places):
        inside = (places[:, :, None] >= begin[:, None, :]) & (
            places[:, :, None] < finish[:, None, :]
        )
        flags = inside.astype(jnp.int32)
        labels = jnp.sum(flags * jnp.arange(slots, dtype=jnp.int32)[None, None, :], axis=2)
        labels = labels + (1 - jnp.sum(flags, axis=2)) * slots
        return (inside.astype(f32), labels.astype(f32))

    def starts(core, stream):
        return [
            (tensor_index ^ chunk if square() else chunk) * local + core * mine
            for chunk in chunk_order(stream)
        ]

    steps = jnp.arange(mine, dtype=jnp.int32)

    def row_places(core):
        return jnp.stack(
            [
                jnp.concatenate([start + steps for start in starts(core, i)])
                for i in range(micro)
            ]
        )

    my_places = tensor_index * local + section * mine + steps
    member, unused = layout(my_places[None, :])
    row_member, row_labels = layout(row_places(section))
    unused, other_labels = layout(row_places(1 - section))
    key_labels = jnp.concatenate([row_labels, other_labels], axis=1)
    head_gate = jnp.einsum("mns,msh->mhn", row_member, head_mask.astype(f32), precision=highest)
    skip = jnp.stack(
        [
            jnp.concatenate(
                [
                    lax.dynamic_slice_in_dim(skip_mask[i], start, mine, 0)
                    for start in starts(section, i)
                ]
            )
            for i in range(micro)
        ]
    ).astype(f32)

    members = jnp.concatenate([member] * 3, axis=2).astype(bf16)
    row_members = jnp.concatenate([row_member] * 3, axis=2).astype(bf16)
    members_t = jnp.transpose(member, (0, 2, 1)).astype(bf16)
    row_count = row_labels.shape[1]
    padded = -(-2 * hc // 128) * 128
    hidden_cols = fc1_w.shape[2]

    def shape(rows, cols, kind):
        return jax.ShapeDtypeStruct((rows, cols), kind)

    latest = [None]
    begun = []

    def after(arrays):
        if latest[0] is None:
            return arrays
        settled = begun[-2] if len(begun) >= 2 else ()
        return lax.optimization_barrier((arrays, latest[0], settled))[0]

    def ends(array):
        latest[0] = array

    def begins(pieces, first):
        begun.append(first)
        return pieces

    def stream(i, x, g, results):
        of_mine = shape(mine, width, f32)
        low_mine = shape(mine, width, bf16)
        low_rows = shape(row_count, width, bf16)
        row_shape = shape(1, mine, f32)
        terms = partial_shapes(row_count, width)
        tokens, tokens_t = members[i], members_t[i]
        kept = []
        first_mine = x
        x = x.astype(f32)
        g = g.astype(f32)
        for b in range(2):
            pieces = begins(*gather_start(first_mine, i))
            yield
            pieces = after(pieces)
            more = [row_members[i], mod[0][i]] if b == 0 else []
            first, query, keyvalue = run(
                functools.partial(qkv_kernel if more == [] else qkv_first_kernel, len(pieces)),
                [low_rows, shape(row_count, hc, bf16), shape(row_count, padded, bf16)],
                *pieces,
                *more,
                wqkv[b],
                name="qkv", vmem=10,
            )
            ends(query)
            other = begins(swap_cores(keyvalue), ())
            yield
            other = after(other)
            mixed, lse, *parts = run(
                functools.partial(attention_forward_kernel, heads),
                [shape(row_count, hc, bf16), shape(heads, row_count, f32), *terms],
                query,
                keyvalue,
                other,
                key_labels[i][None, :],
                head_gate[i],
                wproj[b],
                name="attend", vmem=10,
            )
            ends(mixed)
            pieces = begins(*scatter_start(parts, i))
            yield
            pieces = after(pieces)
            attended, middle, second_mine, rms_attended = run(
                functools.partial(after_attention_kernel, len(pieces)),
                [of_mine, of_mine, low_mine, row_shape],
                *pieces,
                x,
                tokens,
                mod[b][i],
                name="after_attend", vmem=6,
            )
            ends(second_mine)
            pieces = begins(*gather_start(second_mine, i))
            yield
            pieces = after(pieces)
            second, hidden, slope, *parts = run(
                functools.partial(feed_kernel, len(pieces)),
                [
                    low_rows,
                    shape(row_count, hidden_cols, bf16),
                    shape(row_count, hidden_cols, bf16),
                    *terms,
                ],
                *pieces,
                wup[b],
                wdown[b],
                skip[i][None, :],
                name="feed", vmem=7,
            )
            ends(hidden)
            pieces = begins(*scatter_start(parts, i))
            yield
            pieces = after(pieces)
            x_in_block = x
            if b == 0:
                feed, x, rms_feed, first_mine = run(
                    functools.partial(after_feed_kernel, len(pieces), False),
                    [of_mine, of_mine, row_shape, low_mine],
                    *pieces,
                    middle,
                    tokens,
                    mod[b][i],
                    mod[1][i],
                    name="after_feed", vmem=6,
                )
            else:
                feed, x, rms_feed = run(
                    functools.partial(after_feed_kernel, len(pieces), True),
                    [of_mine, of_mine, row_shape],
                    *pieces,
                    middle,
                    tokens,
                    mod[b][i],
                    name="after_feed", vmem=6,
                )
            ends(x)
            kept.append(
                (x_in_block, first, query, keyvalue, other, lse, mixed, attended, middle)
                + (second, hidden, slope, feed)
            )
            results["out", b, i] = x
            results["rms", b, i] = (rms_attended, rms_feed)
        (feed_mine,) = run(upstream_kernel, [low_mine], g, tokens, mod[1][i], name="upstream", vmem=4)
        ends(feed_mine)
        for b in (1, 0):
            x, first, query, keyvalue, other, lse, mixed, attended, middle = kept[b][:9]
            second, hidden, slope, feed = kept[b][9:]
            pieces = begins(*gather_start(feed_mine, i))
            yield
            pieces = after(pieces)
            for name, array in dict(second=second, hidden=hidden, first=first, mixed=mixed).items():
                results[name, b, i] = array
            feed_rows, pre_grad, *parts = run(
                functools.partial(feed_back_kernel, len(pieces)),
                [low_rows, shape(row_count, hidden_cols, bf16), *terms],
                *pieces,
                wup[b],
                wdown[b],
                slope,
                name="feed_back", vmem=7,
            )
            ends(pre_grad)
            results["feed_rows", b, i] = feed_rows
            results["pre_grad", b, i] = pre_grad
            pieces = begins(*scatter_start(parts, i))
            yield
            pieces = after(pieces)
            middle_grad, attn_mine, sums_two = run(
                functools.partial(after_feed_back_kernel, len(pieces)),
                [of_mine, low_mine, shape(slots, 4 * width, f32)],
                *pieces,
                middle,
                g,
                attended,
                feed,
                tokens,
                tokens_t,
                mod[b][i],
                name="after_feed_back", vmem=8,
            )
            ends(attn_mine)
            pieces = begins(*gather_start(attn_mine, i))
            yield
            pieces = after(pieces)
            attn_rows, query_grad, own_grad, other_grad = run(
                functools.partial(attention_back_kernel, len(pieces), heads),
                [
                    low_rows,
                    shape(row_count, hc, bf16),
                    shape(row_count, 2 * hc, f32),
                    shape(row_count, padded, bf16),
                ],
                *pieces,
                wproj[b],
                query,
                keyvalue,
                other,
                key_labels[i][None, :],
                head_gate[i],
                lse,
                name="attend_back", vmem=14,
            )
            ends(query_grad)
            arrived = begins(swap_cores(other_grad), ())
            yield
            arrived = after(arrived)
            qkv_grad, *parts = run(
                qkv_back_kernel,
                [shape(row_count, 3 * hc, bf16), *terms],
                query_grad,
                own_grad,
                arrived,
                wqkv[b],
                name="qkv_back", vmem=5,
            )
            ends(qkv_grad)
            results["attn_rows", b, i] = attn_rows
            results["qkv_grad", b, i] = qkv_grad
            pieces = begins(*scatter_start(parts, i))
            yield
            pieces = after(pieces)
            if b == 1:
                g, sums_one, feed_mine = run(
                    functools.partial(after_attention_back_kernel, len(pieces), False),
                    [of_mine, shape(slots, 2 * width, f32), low_mine],
                    *pieces,
                    x,
                    middle_grad,
                    tokens,
                    tokens_t,
                    mod[b][i],
                    mod[0][i],
                    name="after_attend_back", vmem=8,
                )
            else:
                g, sums_one = run(
                    functools.partial(after_attention_back_kernel, len(pieces), True),
                    [of_mine, shape(slots, 2 * width, f32)],
                    *pieces,
                    x,
                    middle_grad,
                    tokens,
                    tokens_t,
                    mod[b][i],
                    name="after_attend_back", vmem=8,
                )
            ends(g)
            results["grad", b, i] = g
            results["mod", b, i] = jnp.concatenate([sums_one, sums_two], axis=1)

    flag = section.astype(jnp.int32)[None]

    def summed(kernel, name, b, lefts, rights, cols):
        lefts = [array for group in lefts for array in collected(group, b)]
        rights = [array for group in rights for array in collected(group, b)]
        lefts, rights = after((lefts, rights))
        keep, send = weight_sums(
            functools.partial(kernel, micro), flag, lefts, rights, cols, name
        )
        ends(keep)
        results[name, b] = (keep, swap_cores(send))

    def reduced(name, b):
        total = add(*after(results[name, b]), vmem=12)
        ends(total)
        results[name, b] = lax.psum_scatter(total, "dp", scatter_dimension=0, tiled=True)

    def wide(b):
        summed(
            wide_kernel, "wide", b, ("second", "feed_rows"), ("pre_grad", "hidden"), hidden_cols
        )

    def narrow(b):
        summed(
            narrow_kernel, "narrow", b, ("first", "attn_rows"), ("qkv_grad", "mixed"), padded
        )

    def my_rows(array):
        block = lax.dynamic_slice_in_dim(array, section * mine, mine, 1)
        return [block[i] for i in range(micro)]

    results = {}

    def collected(name, b):
        return [results[name, b, i] for i in range(micro)]

    xs = my_rows(x_in)
    gs = my_rows(cotangent)
    running = [stream(i, xs[i], gs[i], results) for i in range(micro)]
    extra = {12: (wide, 1), 15: (narrow, 1), 17: (wide, 0)}
    ready = {13: ("wide", 1), 16: ("narrow", 1), 18: ("wide", 0)}
    settled = {16: ("wide", 1), 19: ("narrow", 1)}
    for step in range(21):
        for i, one in enumerate(running):
            if step == 20 and i == 0:
                narrow(0)
            if step == 20 and i == micro - 1:
                reduced("narrow", 0)
            if step < 21:
                next(one, None)
            behind = step
            if i == 0 and behind in ready:
                reduced(*ready[behind])
            if i == 1 and behind in extra:
                work, b = extra[behind]
                work(b)
            if i == 0 and behind in settled:
                ends((latest[0], results[settled[behind]]))

    out_zero, out_one = collected("out", 0), collected("out", 1)
    back_zero, back_one = collected("grad", 0), collected("grad", 1)
    rms_zero, rms_one = (
        jnp.stack(
            [jnp.concatenate([pair[k] for pair in collected("rms", b)]) for k in range(2)]
        )
        for b in range(2)
    )
    mods_zero, mods_one = (jnp.concatenate(collected("mod", b), axis=0) for b in range(2))
    weights_zero, weights_one = (
        (results["wide", b], results["narrow", b]) for b in range(2)
    )

    residual = jnp.concatenate(to_owner(jnp.stack(out_zero), jnp.stack(out_one)), axis=1)
    input_grad = jnp.concatenate(
        to_owner(jnp.stack(back_zero).astype(bf16), jnp.stack(back_one).astype(bf16)), axis=1
    )
    sublayer_rms = jnp.concatenate(to_owner(rms_zero, rms_one), axis=2)

    mod_sum = choose(mods_zero, mods_one) + swap_cores(choose(mods_one, mods_zero))
    mod_here = scatter_columns(mod_sum.astype(bf16))
    mod_here = lax.optimization_barrier((mod_here, results["wide", 0]))[0]
    mod_all = gather_dp(mod_here)
    condition_all = gather_dp(flat_condition)
    rows_here = width // lax.axis_size("dp")
    condition_here = lax.dynamic_slice_in_dim(condition_all, dp_index * rows_here, rows_here, 2)
    ada_grad = jnp.einsum(
        "psd,pse->de", condition_here, mod_all, preferred_element_type=f32
    )

    wide, narrow = (
        to_owner(zero, one) for zero, one in zip(weights_zero, weights_one)
    )
    up_grad = wide[0].astype(f32)
    down_grad = wide[1].astype(f32).T
    qkv_grad = jnp.stack([narrow[0][:, :hc], narrow[0][:, hc : 2 * hc], narrow[1][:, :hc]]).astype(f32)
    proj_grad = narrow[1][:, hc : 2 * hc].astype(f32).T
    return (
        residual[None],
        input_grad[None],
        sublayer_rms[None],
        ada_grad[None],
        qkv_grad[None],
        proj_grad[None],
        up_grad[None],
        down_grad[None],
    )


def solution(mesh):
    in_specs = (
        P(None, ("dp", "tensor"), None),
        P(None, ("dp", "tensor"), None),
        P(None, "dp", None),
        P(None, "dp"),
        P(None, "dp", "tensor"),
        P(None, "dp"),
        P("section", None, "tensor"),
        P("section", None, None, "tensor"),
        P("section", "tensor", None),
        P("section", None, "tensor"),
        P("section", "tensor", None),
    )
    out_specs = (
        P("section", None, ("dp", "tensor"), None),
        P("section", None, ("dp", "tensor"), None),
        P("section", None, None, ("dp", "tensor")),
        P("section", "dp", "tensor"),
        P("section", None, "dp", "tensor"),
        P("section", "tensor", "dp"),
        P("section", "dp", "tensor"),
        P("section", "tensor", "dp"),
    )
    return jax.shard_map(
        on_device, mesh=mesh, in_specs=in_specs, out_specs=out_specs, check_vma=False
    )
```

```python
import functools
import math

import jax
import jax.numpy as jnp
from jax import lax
from jax.experimental import pallas as pl
from jax.experimental.pallas import tpu as pltpu
from jax.sharding import PartitionSpec as P

highest = lax.Precision.HIGHEST
epsilon = 1e-06
f32 = jnp.float32
bf16 = jnp.bfloat16
log2e = math.log2(math.e)
brief = pl.CostEstimate(flops=1000000000, bytes_accessed=1, transcendentals=0)
lengthy = pl.CostEstimate(flops=9000000000, bytes_accessed=1, transcendentals=0)


def normalize_keep(value):
    centered = value - jnp.mean(value, axis=-1, keepdims=True)
    factor = lax.rsqrt(jnp.mean(centered * centered, axis=-1, keepdims=True) + epsilon)
    return (centered * factor, factor)


def normalize_back(normed, factor, upstream):
    return factor * (
        upstream
        - jnp.mean(upstream, axis=-1, keepdims=True)
        - normed * jnp.mean(upstream * normed, axis=-1, keepdims=True)
    )


def swap_cores(block):
    return lax.ppermute(block, "section", [(0, 1), (1, 0)])


def along_x(block):
    return lax.ppermute(block, "tensor", [(0, 1), (1, 0), (2, 3), (3, 2)])


def along_y(block):
    return lax.ppermute(block, "tensor", [(0, 2), (2, 0), (1, 3), (3, 1)])


def square():
    return lax.axis_size("tensor") == 4


def axes_of(stream):
    return ((along_x, 1), (along_y, 2)) if stream % 2 == 0 else ((along_y, 2), (along_x, 1))


def chunk_order(stream):
    if square():
        (unused, near), (unused, far) = axes_of(stream)
        return [0, far, near, 3]
    return range(lax.axis_size("tensor"))


def halves_kernel(near, far, near_half, far_half):
    half = near_half.shape[0]
    near_half[...] = near[:half, :]
    far_half[...] = far[half:, :]


def gather_start(block, stream):
    if not square():
        return ((lax.all_gather(block, "tensor", axis=0, tiled=True),), ())
    (along, unused), (across, unused) = axes_of(stream)
    near = along(block)
    far = across(block)
    half = block.shape[0] // 2
    near_half, far_half = run(
        halves_kernel,
        [jax.ShapeDtypeStruct((half, block.shape[1]), bf16)] * 2,
        near,
        far,
        name="halves",
        vmem=4,
    )
    return ((block, far, near, across(near_half), along(far_half)), (near_half, far_half))


def assemble(pieces, target):
    begin = 0
    for piece in pieces:
        target[begin : begin + piece.shape[0], :] = piece[...]
        begin += piece.shape[0]


def partial_shapes(rows, width):
    parts = 4 if square() else 1
    return [jax.ShapeDtypeStruct((rows // parts, width), bf16)] * parts


def store_partial(refs, columns, value):
    value = value.astype(bf16)
    if len(refs) == 1:
        refs[0][:, columns] = value
        return
    mine = refs[0].shape[0]
    half = mine // 2
    own, stay, leave_along, leave_across = refs
    own[:, columns] = value[:mine]
    stay[:half, columns] = value[mine : mine + half]
    stay[half:, columns] = value[2 * mine + half : 3 * mine]
    leave_along[:half, columns] = value[2 * mine : 2 * mine + half]
    leave_along[half:, columns] = value[3 * mine : 3 * mine + half]
    leave_across[:half, columns] = value[mine + half : 2 * mine]
    leave_across[half:, columns] = value[3 * mine + half :]


def add_kernel(left, right, out):
    out[...] = (left[...].astype(f32) + right[...].astype(f32)).astype(bf16)


def add(left, right, vmem=4):
    (total,) = run(
        add_kernel, [jax.ShapeDtypeStruct(left.shape, bf16)], left, right, name="add", vmem=vmem
    )
    return total


def add_halves_kernel(stay, first, second, far, near):
    half = far.shape[0]
    far[...] = (stay[:half, :].astype(f32) + first[half:, :].astype(f32)).astype(bf16)
    near[...] = (stay[half:, :].astype(f32) + second[half:, :].astype(f32)).astype(bf16)


def scatter_start(parts, stream):
    if not square():
        total = lax.psum_scatter(parts[0], "tensor", scatter_dimension=0, tiled=True)
        return ((total,), ())
    (along, unused), (across, unused) = axes_of(stream)
    own, stay, leave_along, leave_across = parts
    half = own.shape[0] // 2
    first, second = along(leave_along), across(leave_across)
    far, near = run(
        add_halves_kernel,
        [jax.ShapeDtypeStruct((half, own.shape[1]), bf16)] * 2,
        stay,
        first,
        second,
        name="add_halves",
        vmem=4,
    )
    return ((own, first, second, across(far), along(near)), (far, near))


def scattered(pieces):
    if len(pieces) == 1:
        return pieces[0][...].astype(f32)
    own, first, second, far, near = pieces
    half = far.shape[0]
    upper = own[:half, :].astype(f32) + first[:half, :].astype(f32) + far[...].astype(f32)
    lower = own[half:, :].astype(f32) + second[:half, :].astype(f32) + near[...].astype(f32)
    return jnp.concatenate([upper, lower], axis=0)


def gather_columns(block):
    if not square():
        return lax.all_gather(block, "tensor", axis=1, tiled=True)
    from_x = along_x(block)
    from_y = along_y(block)
    pieces = jnp.stack([block, from_x, from_y, along_x(from_y)])
    here = lax.axis_index("tensor")
    return jnp.concatenate(
        [lax.dynamic_index_in_dim(pieces, here ^ j, 0, keepdims=False) for j in range(4)], axis=1
    )


def scatter_columns(partial):
    if not square():
        return lax.psum_scatter(partial, "tensor", scatter_dimension=1, tiled=True)
    here = lax.axis_index("tensor")
    columns = partial.shape[1] // 4

    def piece(distance):
        return lax.dynamic_slice_in_dim(partial, (here ^ distance) * columns, columns, 1)

    arrived = along_x(jnp.stack([piece(1), piece(3)])).astype(f32)
    passed = along_y((piece(2).astype(f32) + arrived[1]).astype(partial.dtype))
    return (piece(0).astype(f32) + arrived[0] + passed.astype(f32)).astype(partial.dtype)


def gather_dp(block):
    size = lax.axis_size("dp")
    others = [
        lax.ppermute(block, "dp", [(i, (i + step) % size) for i in range(size)])
        for step in range(1, size)
    ]
    return jnp.stack([block] + others)


def dot_last(left, right):
    return lax.dot_general(left, right, (((1,), (1,)), ((), ())), preferred_element_type=f32)


def dot_plain(left, right):
    return lax.dot_general(left, right, (((1,), (0,)), ((), ())), preferred_element_type=f32)


def dot_first(left, right):
    return lax.dot_general(left, right, (((0,), (0,)), ((), ())), preferred_element_type=f32)


def chunks(size, most=384):
    step = most if size % most == 0 else size
    return [slice(begin, begin + step) for begin in range(0, size, step)]


matmuls = ("qkv", "attend", "feed", "feed_back", "attend_back", "qkv_back")


def run(kernel, shapes, *arrays, name, vmem):
    return pl.pallas_call(
        kernel,
        out_shape=tuple(shapes),
        compiler_params=pltpu.CompilerParams(vmem_limit_bytes=vmem * 1024 * 1024),
        cost_estimate=lengthy if name in matmuls else brief,
        name=name,
    )(*arrays)


def block_mod(member, mod, index):
    width = mod.shape[1] // 6
    return dot_plain(member[...], mod[:, index * width : (index + 1) * width])


def slot_sums(member_t, value):
    high = value.astype(bf16)
    low = (value - high.astype(f32)).astype(bf16)
    return dot_plain(member_t[...], high) + dot_plain(member_t[...], low)


def root_mean(value):
    return rows_of([jnp.sqrt(jnp.mean(value * value, axis=1, keepdims=True))])


def first_kernel(x, member, mod, out):
    normed, unused = normalize_keep(x[...])
    out[...] = (normed * (1.0 + block_mod(member, mod, 1)) + block_mod(member, mod, 0)).astype(bf16)


def upstream_kernel(g, member, mod, out):
    out[...] = (g[...] * block_mod(member, mod, 5)).astype(bf16)


def column(row):
    return columns_of(row)[:, :1]


def columns_of(rows):
    count, size = rows.shape
    if count < 8:
        rows = jnp.concatenate([rows, jnp.zeros((8 - count, size), f32)], axis=0)
    return jnp.transpose(rows)


def rows_of(columns):
    size = columns[0].shape[0]
    blank = jnp.zeros((size, 128 - len(columns)), f32)
    return jnp.transpose(jnp.concatenate([*columns, blank], axis=1))[: len(columns), :]


def qkv_first_kernel(count, *refs):
    pieces, (member, mod, weight, rows, query, keyvalue) = refs[:count], refs[count:]
    begin = 0
    for piece in pieces:
        part = slice(begin, begin + piece.shape[0])
        first_kernel(piece[...].astype(f32), member[part, :], mod, rows.at[part, :])
        begin += piece.shape[0]
    project(rows, weight, query, keyvalue)


def qkv_kernel(count, *refs):
    pieces, (weight, rows, query, keyvalue) = refs[:count], refs[count:]
    assemble(pieces, rows)
    project(rows, weight, query, keyvalue)


def project(rows, weight, query, keyvalue):
    size, cols = query.shape
    out = dot_last(rows[...], weight[...]).astype(bf16)
    query[...] = out[:, :cols]
    keyvalue[:, : 2 * cols] = out[:, cols:]
    keyvalue[:, 2 * cols :] = jnp.zeros((size, keyvalue.shape[1] - 2 * cols), bf16)


def attention_forward_kernel(
    heads, query_ref, own_ref, other_ref, label_ref, gate_ref, weight_ref, mixed_ref, lse_ref, *parts
):
    rows, cols = query_ref.shape
    dim = cols // heads
    scale = dim ** (-0.5)
    labels = column(label_ref[:, :rows])
    gates = columns_of(gate_ref[...])
    same = [labels == label_ref[:, :rows], labels == label_ref[:, rows:]]
    mixed = []
    totals = []
    for head in range(heads):
        part = slice(head * dim, (head + 1) * dim)
        value_part = slice(cols + head * dim, cols + (head + 1) * dim)
        query = query_ref[:, part]
        keys = [own_ref[:, part], other_ref[:, part]]
        values = [own_ref[:, value_part], other_ref[:, value_part]]
        scores = [jnp.where(same[j], dot_last(query, keys[j]), -1e30) for j in range(2)]
        peak = jnp.maximum(
            jnp.max(scores[0], axis=1, keepdims=True), jnp.max(scores[1], axis=1, keepdims=True)
        )
        expos = [jnp.exp2((scores[j] - peak) * (scale * log2e)) for j in range(2)]
        total = jnp.sum(expos[0], axis=1, keepdims=True) + jnp.sum(expos[1], axis=1, keepdims=True)
        inverse = 1.0 / total
        out = dot_plain((expos[0] * inverse).astype(bf16), values[0])
        out = out + dot_plain((expos[1] * inverse).astype(bf16), values[1])
        mixed.append((out * gates[:, head : head + 1]).astype(bf16))
        totals.append(peak * scale + jnp.log(total))
    mixed_ref[...] = jnp.concatenate(mixed, axis=1)
    lse_ref[...] = rows_of(totals)
    for columns in chunks(weight_ref.shape[1]):
        store_partial(parts, columns, dot_plain(mixed_ref[...], weight_ref[:, columns]))


def after_attention_kernel(count, *refs):
    pieces = refs[:count]
    x, member, mod, attended_out, middle_out, second_out, rms_out = refs[count:]
    attended = scattered(pieces)
    middle = x[...] + block_mod(member, mod, 2) * attended
    normed, unused = normalize_keep(middle)
    attended_out[...] = attended
    middle_out[...] = middle
    rms_out[...] = root_mean(attended)
    second_out[...] = (
        normed * (1.0 + block_mod(member, mod, 4)) + block_mod(member, mod, 3)
    ).astype(bf16)


def feed_kernel(count, *refs):
    pieces = refs[:count]
    up, down, skip, rows, hidden, slope, *parts = refs[count:]
    assemble(pieces, rows)
    inner = math.sqrt(2 / math.pi)
    half_skip = 0.5 * column(skip[...])
    for columns in chunks(up.shape[1]):
        pre = dot_plain(rows[...], up[:, columns])
        square_pre = pre * pre
        tanh = jnp.tanh(inner * pre * (1.0 + 0.044715 * square_pre))
        half_gate = half_skip * (1.0 + tanh)
        hidden[:, columns] = (pre * half_gate).astype(bf16)
        slope[:, columns] = (
            half_gate * (1.0 + pre * (1.0 - tanh) * (inner * (1.0 + 3 * 0.044715 * square_pre)))
        ).astype(bf16)
    for columns in chunks(down.shape[1]):
        store_partial(parts, columns, dot_plain(hidden[...], down[:, columns]))


def after_feed_kernel(count, last, *refs):
    pieces = refs[:count]
    middle, member, mod, *rest = refs[count:]
    feed = scattered(pieces)
    out = middle[...] + block_mod(member, mod, 5) * feed
    if last:
        feed_out, x_out, rms_out = rest
    else:
        next_mod, feed_out, x_out, rms_out, first_out = rest
        first_kernel(out, member, next_mod, first_out)
    feed_out[...] = feed
    x_out[...] = out
    rms_out[...] = root_mean(feed)


def feed_back_kernel(count, *refs):
    pieces = refs[:count]
    up, down, slope, rows, pre_grad, *parts = refs[count:]
    assemble(pieces, rows)
    for columns in chunks(up.shape[1]):
        hidden_grad = dot_last(rows[...], down[columns, :])
        pre_grad[:, columns] = (hidden_grad * slope[:, columns].astype(f32)).astype(bf16)
    for columns in chunks(up.shape[0]):
        store_partial(parts, columns, dot_last(pre_grad[...], up[columns, :]))


def after_feed_back_kernel(count, *refs):
    pieces = refs[:count]
    middle, g, attended, feed, member, member_t, mod, grad_out, attn_out, sums = refs[count:]
    width = middle.shape[1]
    second_grad = scattered(pieces)
    normed, factor = normalize_keep(middle[...])
    middle_grad = g[...] + normalize_back(
        normed, factor, second_grad * (1.0 + block_mod(member, mod, 4))
    )
    grad_out[...] = middle_grad
    attn_out[...] = (middle_grad * block_mod(member, mod, 2)).astype(bf16)
    sums[:, :width] = slot_sums(member_t, middle_grad * attended[...])
    sums[:, width : 2 * width] = slot_sums(member_t, second_grad)
    sums[:, 2 * width : 3 * width] = slot_sums(member_t, second_grad * normed)
    sums[:, 3 * width :] = slot_sums(member_t, g[...] * feed[...])


def attention_back_kernel(count, heads, *refs):
    pieces = refs[:count]
    (
        weight_ref,
        query_ref,
        own_ref,
        other_ref,
        label_ref,
        gate_ref,
        lse_ref,
        upstream_rows,
        query_grad_ref,
        own_grad_ref,
        other_grad_ref,
    ) = refs[count:]
    assemble(pieces, upstream_rows)
    rows, cols = query_ref.shape
    dim = cols // heads
    scale = dim ** (-0.5)
    labels = label_ref[:, :rows]
    gates = columns_of(gate_ref[...])
    mixed_grad = dot_last(upstream_rows[...], weight_ref[...]).astype(bf16).astype(f32)
    same = [column(labels) == labels, column(label_ref[:, rows:]) == labels]
    query_grads = []
    key_grads = [[], []]
    value_grads = [[], []]
    for head in range(heads):
        part = slice(head * dim, (head + 1) * dim)
        value_part = slice(cols + head * dim, cols + (head + 1) * dim)
        query = query_ref[:, part]
        keys = [own_ref[:, part], other_ref[:, part]]
        values = [own_ref[:, value_part], other_ref[:, value_part]]
        upstream = (mixed_grad[:, part] * gates[:, head : head + 1]).astype(bf16)
        lse = lse_ref[head : head + 1, :] * log2e
        weights = []
        weight_grads = []
        for j in range(2):
            scores = jnp.where(same[j], dot_last(keys[j], query) * (scale * log2e), -1e30)
            weights.append(jnp.exp2(scores - lse))
            weight_grads.append(dot_last(values[j], upstream))
            value_grads[j].append(dot_plain(weights[j].astype(bf16), upstream))
        delta = jnp.sum(weights[0] * weight_grads[0], axis=0, keepdims=True)
        delta = delta + jnp.sum(weights[1] * weight_grads[1], axis=0, keepdims=True)
        query_grad = None
        for j in range(2):
            score_grad = (weights[j] * (weight_grads[j] - delta)).astype(bf16)
            key_grads[j].append(dot_plain(score_grad, query) * scale)
            term = dot_first(score_grad, keys[j])
            query_grad = term if query_grad is None else query_grad + term
        query_grads.append((query_grad * scale).astype(bf16))
    query_grad_ref[...] = jnp.concatenate(query_grads, axis=1)
    own_grad_ref[...] = jnp.concatenate(key_grads[0] + value_grads[0], axis=1)
    other_grad_ref[:, : 2 * cols] = jnp.concatenate(
        key_grads[1] + value_grads[1], axis=1
    ).astype(bf16)
    other_grad_ref[:, 2 * cols :] = jnp.zeros((rows, other_grad_ref.shape[1] - 2 * cols), bf16)


def qkv_back_kernel(query_grad, own_grad, arrived, weight, grad, *parts):
    cols = own_grad.shape[1]
    total = own_grad[...] + arrived[:, :cols].astype(f32)
    grad[...] = jnp.concatenate([query_grad[...], total.astype(bf16)], axis=1)
    for columns in chunks(weight.shape[1]):
        store_partial(parts, columns, dot_plain(grad[...], weight[:, columns]))


def after_attention_back_kernel(count, last, *refs):
    pieces = refs[:count]
    x, middle_grad, member, member_t, mod, *rest = refs[count:]
    width = x.shape[1]
    first_grad = scattered(pieces)
    normed, factor = normalize_keep(x[...])
    out = middle_grad[...] + normalize_back(
        normed, factor, first_grad * (1.0 + block_mod(member, mod, 1))
    )
    if last:
        grad_out, sums = rest
    else:
        next_mod, grad_out, sums, feed_out = rest
        upstream_kernel(out, member, next_mod, feed_out)
    grad_out[...] = out
    sums[:, :width] = slot_sums(member_t, first_grad)
    sums[:, width:] = slot_sums(member_t, first_grad * normed)


def wide_kernel(count, flag, *refs):
    seconds, uppers, pres, hiddens = (refs[k * count : (k + 1) * count] for k in range(4))
    keep, send = refs[4 * count :]
    first_core = flag[0] == 0
    for columns in chunks(keep.shape[1]):
        up = sum(dot_first(a[...], b[:, columns]) for a, b in zip(seconds, pres)).astype(bf16)
        down = sum(dot_first(a[...], b[:, columns]) for a, b in zip(uppers, hiddens)).astype(bf16)
        keep[:, columns] = jnp.where(first_core, up, down)
        send[:, columns] = jnp.where(first_core, down, up)


def narrow_kernel(count, flag, *refs):
    firsts, uppers, grads, mixeds = (refs[k * count : (k + 1) * count] for k in range(4))
    keep, send = refs[4 * count :]
    first_core = flag[0] == 0
    qkv = sum(dot_first(a[...], b[...]) for a, b in zip(firsts, grads)).astype(bf16)
    proj = sum(dot_first(a[...], b[...]) for a, b in zip(uppers, mixeds)).astype(bf16)
    cols = proj.shape[1]
    fill = [jnp.zeros((qkv.shape[0], keep.shape[1] - 2 * cols), bf16)]
    if not fill[0].shape[1]:
        fill = []
    zero = jnp.concatenate([qkv[:, : 2 * cols], *fill], axis=1)
    one = jnp.concatenate([qkv[:, 2 * cols :], proj, *fill], axis=1)
    keep[...] = jnp.where(first_core, zero, one)
    send[...] = jnp.where(first_core, one, zero)


def weight_sums(kernel, flag, lefts, rights, width, name):
    rows, depth = lefts[0].shape
    step = chunks(depth)[0].stop

    def whole(array):
        return pl.BlockSpec(array.shape, lambda j: (0, 0))

    return pl.pallas_call(
        kernel,
        grid=(depth // step,),
        in_specs=[
            pl.BlockSpec(memory_space=pltpu.SMEM),
            *(pl.BlockSpec((rows, step), lambda j: (0, j)) for unused in lefts),
            *(whole(array) for array in rights),
        ],
        out_specs=[pl.BlockSpec((step, width), lambda j: (j, 0))] * 2,
        out_shape=[jax.ShapeDtypeStruct((depth, width), bf16)] * 2,
        compiler_params=pltpu.CompilerParams(vmem_limit_bytes=32 * 1024 * 1024),
        cost_estimate=lengthy,
        name=name,
    )(flag, *lefts, *rights)


def three_terms(value):
    high = lax.reduce_precision(value, 8, 7)
    rest = value - high
    low = lax.reduce_precision(rest, 8, 7)
    return jnp.concatenate([high, low, rest - low], axis=0).astype(bf16)


def on_device(
    x_in, cotangent, cond, crop_len, head_mask, skip_mask, ada_w, qkv_w, proj_w, fc1_w, fc2_w
):
    micro, local, width = x_in.shape
    row = skip_mask.shape[1]
    slots = crop_len.shape[1]
    heads = head_mask.shape[2]
    mine = local // 2
    section = lax.axis_index("section")
    tensor_index = lax.axis_index("tensor")
    dp_index = lax.axis_index("dp")
    first_core = section == 0

    def choose(zero, one):
        return jax.tree.map(lambda a, b: jnp.where(first_core, a, b), zero, one)

    def both_blocks(own):
        other = swap_cores(own)
        return (choose(own, other), choose(other, own))

    def to_owner(zero, one):
        own = choose(zero, one)
        other = swap_cores(choose(one, zero))
        return (choose(own, other), choose(other, own))

    hc = qkv_w.shape[3]
    wqkv = both_blocks(jnp.transpose(qkv_w[0], (0, 2, 1)).reshape(3 * hc, width))
    wproj = both_blocks(proj_w[0])
    wup = both_blocks(fc1_w[0])
    wdown = both_blocks(fc2_w[0])

    condition = jax.nn.silu(cond.astype(f32)).astype(bf16)
    flat_condition = condition.reshape(micro * slots, width)
    mod_local = jnp.dot(flat_condition, ada_w[0], preferred_element_type=f32)
    modulation = both_blocks(gather_columns(mod_local))
    mod = [
        [three_terms(modulation[b][i * slots : (i + 1) * slots]) for i in range(micro)]
        for b in range(2)
    ]

    finish = jnp.cumsum(crop_len, axis=1)
    begin = finish - crop_len

    def layout(places):
        inside = (places[:, :, None] >= begin[:, None, :]) & (
            places[:, :, None] < finish[:, None, :]
        )
        flags = inside.astype(jnp.int32)
        labels = jnp.sum(flags * jnp.arange(slots, dtype=jnp.int32)[None, None, :], axis=2)
        labels = labels + (1 - jnp.sum(flags, axis=2)) * slots
        return (inside.astype(f32), labels.astype(f32))

    def starts(core, stream):
        return [
            (tensor_index ^ chunk if square() else chunk) * local + core * mine
            for chunk in chunk_order(stream)
        ]

    steps = jnp.arange(mine, dtype=jnp.int32)

    def row_places(core):
        return jnp.stack(
            [
                jnp.concatenate([start + steps for start in starts(core, i)])
                for i in range(micro)
            ]
        )

    my_places = tensor_index * local + section * mine + steps
    member, unused = layout(my_places[None, :])
    row_member, row_labels = layout(row_places(section))
    unused, other_labels = layout(row_places(1 - section))
    key_labels = jnp.concatenate([row_labels, other_labels], axis=1)
    head_gate = jnp.einsum("mns,msh->mhn", row_member, head_mask.astype(f32), precision=highest)
    skip = jnp.stack(
        [
            jnp.concatenate(
                [
                    lax.dynamic_slice_in_dim(skip_mask[i], start, mine, 0)
                    for start in starts(section, i)
                ]
            )
            for i in range(micro)
        ]
    ).astype(f32)

    members = jnp.concatenate([member] * 3, axis=2).astype(bf16)
    row_members = jnp.concatenate([row_member] * 3, axis=2).astype(bf16)
    members_t = jnp.transpose(member, (0, 2, 1)).astype(bf16)
    row_count = row_labels.shape[1]
    padded = -(-2 * hc // 128) * 128
    hidden_cols = fc1_w.shape[2]

    def shape(rows, cols, kind):
        return jax.ShapeDtypeStruct((rows, cols), kind)

    latest = [None]
    begun = []

    def after(arrays):
        if latest[0] is None:
            return arrays
        settled = begun[-2] if len(begun) >= 2 else ()
        return lax.optimization_barrier((arrays, latest[0], settled))[0]

    def ends(array):
        latest[0] = array

    def begins(pieces, first):
        begun.append(first)
        return pieces

    def stream(i, x, g, results):
        of_mine = shape(mine, width, f32)
        low_mine = shape(mine, width, bf16)
        low_rows = shape(row_count, width, bf16)
        row_shape = shape(1, mine, f32)
        terms = partial_shapes(row_count, width)
        tokens, tokens_t = members[i], members_t[i]
        kept = []
        first_mine = x
        x = x.astype(f32)
        g = g.astype(f32)
        for b in range(2):
            pieces = begins(*gather_start(first_mine, i))
            yield
            pieces = after(pieces)
            more = [row_members[i], mod[0][i]] if b == 0 else []
            first, query, keyvalue = run(
                functools.partial(qkv_kernel if more == [] else qkv_first_kernel, len(pieces)),
                [low_rows, shape(row_count, hc, bf16), shape(row_count, padded, bf16)],
                *pieces,
                *more,
                wqkv[b],
                name="qkv", vmem=10,
            )
            ends(query)
            other = begins(swap_cores(keyvalue), ())
            yield
            other = after(other)
            mixed, lse, *parts = run(
                functools.partial(attention_forward_kernel, heads),
                [shape(row_count, hc, bf16), shape(heads, row_count, f32), *terms],
                query,
                keyvalue,
                other,
                key_labels[i][None, :],
                head_gate[i],
                wproj[b],
                name="attend", vmem=10,
            )
            ends(mixed)
            pieces = begins(*scatter_start(parts, i))
            yield
            pieces = after(pieces)
            attended, middle, second_mine, rms_attended = run(
                functools.partial(after_attention_kernel, len(pieces)),
                [of_mine, of_mine, low_mine, row_shape],
                *pieces,
                x,
                tokens,
                mod[b][i],
                name="after_attend", vmem=6,
            )
            ends(second_mine)
            pieces = begins(*gather_start(second_mine, i))
            yield
            pieces = after(pieces)
            second, hidden, slope, *parts = run(
                functools.partial(feed_kernel, len(pieces)),
                [
                    low_rows,
                    shape(row_count, hidden_cols, bf16),
                    shape(row_count, hidden_cols, bf16),
                    *terms,
                ],
                *pieces,
                wup[b],
                wdown[b],
                skip[i][None, :],
                name="feed", vmem=7,
            )
            ends(hidden)
            pieces = begins(*scatter_start(parts, i))
            yield
            pieces = after(pieces)
            x_in_block = x
            if b == 0:
                feed, x, rms_feed, first_mine = run(
                    functools.partial(after_feed_kernel, len(pieces), False),
                    [of_mine, of_mine, row_shape, low_mine],
                    *pieces,
                    middle,
                    tokens,
                    mod[b][i],
                    mod[1][i],
                    name="after_feed", vmem=6,
                )
            else:
                feed, x, rms_feed = run(
                    functools.partial(after_feed_kernel, len(pieces), True),
                    [of_mine, of_mine, row_shape],
                    *pieces,
                    middle,
                    tokens,
                    mod[b][i],
                    name="after_feed", vmem=6,
                )
            ends(x)
            kept.append(
                (x_in_block, first, query, keyvalue, other, lse, mixed, attended, middle)
                + (second, hidden, slope, feed)
            )
            results["out", b, i] = x
            results["rms", b, i] = (rms_attended, rms_feed)
        (feed_mine,) = run(upstream_kernel, [low_mine], g, tokens, mod[1][i], name="upstream", vmem=4)
        ends(feed_mine)
        for b in (1, 0):
            x, first, query, keyvalue, other, lse, mixed, attended, middle = kept[b][:9]
            second, hidden, slope, feed = kept[b][9:]
            pieces = begins(*gather_start(feed_mine, i))
            yield
            pieces = after(pieces)
            for name, array in dict(second=second, hidden=hidden, first=first, mixed=mixed).items():
                results[name, b, i] = array
            feed_rows, pre_grad, *parts = run(
                functools.partial(feed_back_kernel, len(pieces)),
                [low_rows, shape(row_count, hidden_cols, bf16), *terms],
                *pieces,
                wup[b],
                wdown[b],
                slope,
                name="feed_back", vmem=7,
            )
            ends(pre_grad)
            results["feed_rows", b, i] = feed_rows
            results["pre_grad", b, i] = pre_grad
            pieces = begins(*scatter_start(parts, i))
            yield
            pieces = after(pieces)
            middle_grad, attn_mine, sums_two = run(
                functools.partial(after_feed_back_kernel, len(pieces)),
                [of_mine, low_mine, shape(slots, 4 * width, f32)],
                *pieces,
                middle,
                g,
                attended,
                feed,
                tokens,
                tokens_t,
                mod[b][i],
                name="after_feed_back", vmem=8,
            )
            ends(attn_mine)
            pieces = begins(*gather_start(attn_mine, i))
            yield
            pieces = after(pieces)
            attn_rows, query_grad, own_grad, other_grad = run(
                functools.partial(attention_back_kernel, len(pieces), heads),
                [
                    low_rows,
                    shape(row_count, hc, bf16),
                    shape(row_count, 2 * hc, f32),
                    shape(row_count, padded, bf16),
                ],
                *pieces,
                wproj[b],
                query,
                keyvalue,
                other,
                key_labels[i][None, :],
                head_gate[i],
                lse,
                name="attend_back", vmem=14,
            )
            ends(query_grad)
            arrived = begins(swap_cores(other_grad), ())
            yield
            arrived = after(arrived)
            qkv_grad, *parts = run(
                qkv_back_kernel,
                [shape(row_count, 3 * hc, bf16), *terms],
                query_grad,
                own_grad,
                arrived,
                wqkv[b],
                name="qkv_back", vmem=5,
            )
            ends(qkv_grad)
            results["attn_rows", b, i] = attn_rows
            results["qkv_grad", b, i] = qkv_grad
            pieces = begins(*scatter_start(parts, i))
            yield
            pieces = after(pieces)
            if b == 1:
                g, sums_one, feed_mine = run(
                    functools.partial(after_attention_back_kernel, len(pieces), False),
                    [of_mine, shape(slots, 2 * width, f32), low_mine],
                    *pieces,
                    x,
                    middle_grad,
                    tokens,
                    tokens_t,
                    mod[b][i],
                    mod[0][i],
                    name="after_attend_back", vmem=8,
                )
            else:
                g, sums_one = run(
                    functools.partial(after_attention_back_kernel, len(pieces), True),
                    [of_mine, shape(slots, 2 * width, f32)],
                    *pieces,
                    x,
                    middle_grad,
                    tokens,
                    tokens_t,
                    mod[b][i],
                    name="after_attend_back", vmem=8,
                )
            ends(g)
            results["grad", b, i] = g
            results["mod", b, i] = jnp.concatenate([sums_one, sums_two], axis=1)

    flag = section.astype(jnp.int32)[None]

    def summed(kernel, name, b, lefts, rights, cols):
        lefts = [array for group in lefts for array in collected(group, b)]
        rights = [array for group in rights for array in collected(group, b)]
        lefts, rights = after((lefts, rights))
        keep, send = weight_sums(
            functools.partial(kernel, micro), flag, lefts, rights, cols, name
        )
        ends(keep)
        results[name, b] = (keep, swap_cores(send))

    def reduced(name, b):
        total = add(*after(results[name, b]), vmem=12)
        ends(total)
        results[name, b] = lax.psum_scatter(total, "dp", scatter_dimension=0, tiled=True)

    def wide(b):
        summed(
            wide_kernel, "wide", b, ("second", "feed_rows"), ("pre_grad", "hidden"), hidden_cols
        )

    def narrow(b):
        summed(
            narrow_kernel, "narrow", b, ("first", "attn_rows"), ("qkv_grad", "mixed"), padded
        )

    def my_rows(array):
        block = lax.dynamic_slice_in_dim(array, section * mine, mine, 1)
        return [block[i] for i in range(micro)]

    results = {}

    def collected(name, b):
        return [results[name, b, i] for i in range(micro)]

    xs = my_rows(x_in)
    gs = my_rows(cotangent)
    running = [stream(i, xs[i], gs[i], results) for i in range(micro)]
    extra = {12: (wide, 1), 15: (narrow, 1), 17: (wide, 0)}
    ready = {13: ("wide", 1), 16: ("narrow", 1), 18: ("wide", 0)}
    settled = {16: ("wide", 1), 19: ("narrow", 1)}
    for step in range(21):
        for i, one in enumerate(running):
            if step == 20 and i == 0:
                narrow(0)
            if step == 20 and i == micro - 1:
                reduced("narrow", 0)
            if step < 21:
                next(one, None)
            behind = step
            if i == 0 and behind in ready:
                reduced(*ready[behind])
            if i == (1 if extra.get(behind, (wide,))[0] is wide else 0) and behind in extra:
                work, b = extra[behind]
                work(b)
            if i == 0 and behind in settled:
                ends((latest[0], results[settled[behind]]))

    out_zero, out_one = collected("out", 0), collected("out", 1)
    back_zero, back_one = collected("grad", 0), collected("grad", 1)
    rms_zero, rms_one = (
        jnp.stack(
            [jnp.concatenate([pair[k] for pair in collected("rms", b)]) for k in range(2)]
        )
        for b in range(2)
    )
    mods_zero, mods_one = (jnp.concatenate(collected("mod", b), axis=0) for b in range(2))
    weights_zero, weights_one = (
        (results["wide", b], results["narrow", b]) for b in range(2)
    )

    residual = jnp.concatenate(to_owner(jnp.stack(out_zero), jnp.stack(out_one)), axis=1)
    input_grad = jnp.concatenate(
        to_owner(jnp.stack(back_zero).astype(bf16), jnp.stack(back_one).astype(bf16)), axis=1
    )
    sublayer_rms = jnp.concatenate(to_owner(rms_zero, rms_one), axis=2)

    mod_sum = choose(mods_zero, mods_one) + swap_cores(choose(mods_one, mods_zero))
    mod_here = scatter_columns(mod_sum.astype(bf16))
    mod_here = lax.optimization_barrier((mod_here, results["wide", 0]))[0]
    mod_all = gather_dp(mod_here)
    condition_all = gather_dp(flat_condition)
    rows_here = width // lax.axis_size("dp")
    condition_here = lax.dynamic_slice_in_dim(condition_all, dp_index * rows_here, rows_here, 2)
    ada_grad = jnp.einsum(
        "psd,pse->de", condition_here, mod_all, preferred_element_type=f32
    )

    wide, narrow = (
        to_owner(zero, one) for zero, one in zip(weights_zero, weights_one)
    )
    up_grad = wide[0].astype(f32)
    down_grad = wide[1].astype(f32).T
    qkv_grad = jnp.stack([narrow[0][:, :hc], narrow[0][:, hc : 2 * hc], narrow[1][:, :hc]]).astype(f32)
    proj_grad = narrow[1][:, hc : 2 * hc].astype(f32).T
    return (
        residual[None],
        input_grad[None],
        sublayer_rms[None],
        ada_grad[None],
        qkv_grad[None],
        proj_grad[None],
        up_grad[None],
        down_grad[None],
    )


def solution(mesh):
    in_specs = (
        P(None, ("dp", "tensor"), None),
        P(None, ("dp", "tensor"), None),
        P(None, "dp", None),
        P(None, "dp"),
        P(None, "dp", "tensor"),
        P(None, "dp"),
        P("section", None, "tensor"),
        P("section", None, None, "tensor"),
        P("section", "tensor", None),
        P("section", None, "tensor"),
        P("section", "tensor", None),
    )
    out_specs = (
        P("section", None, ("dp", "tensor"), None),
        P("section", None, ("dp", "tensor"), None),
        P("section", None, None, ("dp", "tensor")),
        P("section", "dp", "tensor"),
        P("section", None, "dp", "tensor"),
        P("section", "tensor", "dp"),
        P("section", "dp", "tensor"),
        P("section", "tensor", "dp"),
    )
    return jax.shard_map(
        on_device, mesh=mesh, in_specs=in_specs, out_specs=out_specs, check_vma=False
    )
```
